256 devices in a mesh: dp: 32 (over z, y), fsdp: 8 (over x, core).
Axes of the slice: x: 4, y: 4, z: 8, core: 2. Of those that a mesh axis runs over, the one named last changes fastest.
Arguments:
- grads: bfloat16 [32, 2, 1792, 2048], P('dp', None, 'fsdp'), may hold values from -16.5 to 16.5
- errors: float32 [32, 2, 1792, 2048], P('dp', None, 'fsdp'), may hold values from -4 to 4
- q_prev: float32 [2, 32, 2048], replicated, may hold values from -0.125 to 0.125
- moment1: float32 [2, 28672, 128], P(None, ('fsdp', 'dp')), may hold values from -1.5 to 1.5
- moment2: float32 [2, 28672, 128], P(None, ('fsdp', 'dp')), may hold values from 0.001 to 0.1
Outputs:
- new_errors: float32 [32, 2, 1792, 2048], P('dp', None, 'fsdp')
- new_moment1: float32 [2, 28672, 128], P(None, ('fsdp', 'dp'))
- new_moment2: float32 [2, 28672, 128], P(None, ('fsdp', 'dp'))
- update: bfloat16 [2, 28672, 128], P(None, ('fsdp', 'dp'))
- q_next: float32 [2, 32, 2048], replicated
The draws below stay inside these ranges and needn't reach their ends.
All inputs are finite; a program needn't handle non-finite values.
Results may differ from the reference program's by a relative error of at most 0.001.
Values sent between devices are 32-bit elements; how exact they have to be, the bound alone decides.
No kernel may reach another device: no remote copies, remote signals or barrier semaphores. Data moves between devices by JAX's collectives and lax.ppermute only.
A program may use at most 64 MiB of HBM per device.

```python
import math
import jax
import jax.numpy as jnp
from jax import lax

D = 1792
KV = 2048
RANK = 32
FLAT = 28672
N_DP = 32


def draw_grads(key, part):
    key = jax.random.fold_in(key, 11)
    first, second, third = jax.random.split(key, 3)
    common = jax.random.truncated_normal(first, -3.0, 3.0, (1, 2, D, KV), jnp.float32)
    noise = 0.5 * jax.random.truncated_normal(second, -3.0, 3.0, (N_DP, 2, D, KV), jnp.float32)
    scales = jnp.exp(jax.random.uniform(third, (1, 2, 1, KV), jnp.float32, math.log(0.2), math.log(5.0)))
    return (common * scales + noise).astype(jnp.bfloat16)


def block_scale(rng, dims, cuts, low, largest):
    def one(axis_at, shards_of):
        steps = jax.random.uniform(jax.random.fold_in(jax.random.fold_in(rng, 6), axis_at), (shards_of,), jnp.float32, low / len(cuts), largest / len(cuts))
        return jnp.repeat(jnp.exp(steps), dims[axis_at] // shards_of).reshape((-1,) + (1,) * (len(dims) - axis_at - 1))

    gain = one(*cuts[0])
    for cut in cuts[1:]:
        gain = gain * one(*cut)
    return gain


def gaussian(stream_key, extent, deviation, most, pieces=(), dtype=jnp.bfloat16):
    array = deviation * jax.random.normal(stream_key, extent, jnp.float32)
    if pieces:
        array = array * block_scale(stream_key, extent, pieces, -0.22, 0.18)
    return jnp.clip(array, -most, most).astype(dtype)


def setup_inputs(seed: int = 0) -> dict:
    splits = jax.random.split(jax.random.key(seed), 6)
    return {
        "grads": draw_grads(jax.random.fold_in(splits[5], 71), 0),
        "errors": gaussian(splits[1], (N_DP, 2, D, KV), 0.3, 4.0, ((0, 32), (2, 8)), jnp.float32),
        "q_prev": gaussian(splits[2], (2, RANK, KV), KV ** -0.5, 0.125, (), jnp.float32),
        "moment1": gaussian(splits[3], (2, FLAT, 128), 0.1, 1.5, ((1, 256),), jnp.float32),
        "moment2": jnp.clip(jnp.exp(math.log(0.1) - 4.6051702 * jax.random.uniform(splits[4], (2, FLAT, 128), jnp.float32) ** block_scale(splits[4], (2, FLAT, 128), ((1, 256),), -0.2, 0.2)), 0.001, 0.1),
    }


def reference(grads, errors, q_prev, moment1, moment2):
    highest = lax.Precision.HIGHEST
    full = grads.astype(jnp.float32) + errors
    p_terms = jnp.einsum('wmdk,mrk->wmrd', full, q_prev, precision=highest)
    p_mean = lax.optimization_barrier(jnp.sum(p_terms, axis=0)) / N_DP
    gram = jnp.einsum('mrd,msd->mrs', p_mean, p_mean, precision=highest)
    lower = jnp.linalg.cholesky(gram)
    p_hat = jax.scipy.linalg.solve_triangular(lower, p_mean, lower=True)
    q_terms = jnp.einsum('wmdk,mrd->wmrk', full, p_hat, precision=highest)
    q_next = lax.optimization_barrier(jnp.sum(q_terms, axis=0)) / N_DP
    approx = jnp.einsum('mrd,mrk->mdk', p_hat, q_next, precision=highest)
    new_errors = full - approx[None]
    flat = approx.reshape(2, FLAT, 128)
    new_moment1 = 0.9 * moment1 + 0.1 * flat
    new_moment2 = 0.95 * moment2 + 0.05 * flat * flat
    update = (new_moment1 / (jnp.sqrt(new_moment2) + 1e-08)).astype(jnp.bfloat16)
    return (new_errors, new_moment1, new_moment2, update, q_next)
```

```python
import functools

import jax
import jax.numpy as jnp
from jax import lax
from jax.experimental import pallas as pl
from jax.experimental.pallas import tpu as pltpu
from jax.sharding import Mesh, PartitionSpec as P

F32 = jnp.float32
BF16 = jnp.bfloat16
RANK = 32
LANES = 128
VMEM_LIMIT = 24 * 2**20


def split(x):
    head = x.astype(BF16)
    return head, (x - head.astype(F32)).astype(BF16)


def dot(a, b, dims, precision=None):
    return lax.dot_general(a, b, (dims, ((), ())), precision=precision, preferred_element_type=F32)


def pack(square):
    return jnp.concatenate([square[8 * i : 8 * i + 8] for i in range(4)], axis=1)


def unpack(packed):
    return jnp.concatenate([packed[:, 32 * i : 32 * i + 32] for i in range(4)], axis=0)


def left_kernel(grads_ref, errors_ref, q_ref, full_ref, p_ref):
    m, step = pl.program_id(0), pl.program_id(1)
    full = grads_ref[0, 0].astype(F32) + errors_ref[0, 0]
    width = full.shape[1]
    full_ref[m, :, pl.ds(pl.multiple_of(step * width, width), width)] = full
    f_hi, f_lo = split(full)
    q_hi, q_lo = split(q_ref[0])
    wide = dot(jnp.concatenate([q_hi, q_lo], axis=0), f_hi, ((1,), (1,)))
    part = wide[:RANK] + wide[RANK:] + dot(q_hi, f_lo, ((1,), (1,)))

    @pl.when(step == 0)
    def _():
        p_ref[0] = part

    @pl.when(step > 0)
    def _():
        p_ref[0] += part


def left_factors(grads, errors, q_prev, blocks=2):
    _, projections, rows, columns = grads.shape
    width = columns // blocks
    return pl.pallas_call(
        left_kernel,
        grid=(projections, blocks),
        in_specs=[
            pl.BlockSpec((1, 1, rows, width), lambda m, k: (0, m, 0, k)),
            pl.BlockSpec((1, 1, rows, width), lambda m, k: (0, m, 0, k)),
            pl.BlockSpec((1, RANK, width), lambda m, k: (m, 0, k)),
        ],
        out_specs=[
            pl.BlockSpec(memory_space=pltpu.VMEM),
            pl.BlockSpec((1, RANK, rows), lambda m, k: (m, 0, 0)),
        ],
        out_shape=[
            jax.ShapeDtypeStruct((projections, rows, columns), F32),
            jax.ShapeDtypeStruct((projections, RANK, rows), F32),
        ],
        compiler_params=pltpu.CompilerParams(vmem_limit_bytes=VMEM_LIMIT),
        name="left_factors",
    )(grads, errors, q_prev)


def right_kernel(replicas, p_ref, full_ref, out_ref):
    projections, _, columns = full_ref.shape
    tiles = columns // LANES
    group = 4
    for m in range(projections):
        p = p_ref[m] * (1.0 / replicas)
        p_hi, p_lo = split(p)
        both = jnp.concatenate([p_hi, p_lo], axis=0)
        gram = pack(dot(p, p, ((1,), (1,)), lax.Precision.HIGHEST))
        for first in range(0, tiles, group):
            f_hi, f_lo = split(full_ref[m, :, first * LANES : (first + group) * LANES])
            wide = dot(both, f_hi, ((1,), (0,)))
            q = wide[:RANK] + wide[RANK:] + dot(p_hi, f_lo, ((1,), (0,)))
            for j in range(group):
                piece = m * tiles + first + j
                out_ref[piece, :RANK, :] = q[:, j * LANES : (j + 1) * LANES]
                out_ref[piece, RANK:, :] = gram


def right_terms(p_sum, full, replicas):
    projections, _, columns = full.shape
    return pl.pallas_call(
        functools.partial(right_kernel, replicas),
        in_specs=[pl.BlockSpec(memory_space=pltpu.VMEM)] * 2,
        out_specs=pl.BlockSpec(memory_space=pltpu.VMEM),
        out_shape=jax.ShapeDtypeStruct((projections * columns // LANES, RANK + 8, LANES), F32),
        compiler_params=pltpu.CompilerParams(vmem_limit_bytes=VMEM_LIMIT),
        name="right_terms",
    )(p_sum, full)


def factor_kernel(copies, sum_ref, out_ref):
    gram = unpack(sum_ref[RANK:, :]) * (1.0 / copies)
    row = lax.broadcasted_iota(jnp.int32, (RANK, RANK), 0)
    column = lax.broadcasted_iota(jnp.int32, (RANK, RANK), 1)
    work = jnp.concatenate([gram, (row == column).astype(F32)], axis=1)
    below = lax.broadcasted_iota(jnp.int32, (RANK, 2 * RANK), 0)
    scale = jnp.zeros((RANK, 1), F32)
    first = lax.broadcasted_iota(jnp.int32, (RANK, 1), 0)
    for k in range(RANK):
        top = work[k : k + 1, :]
        pivot = work[k : k + 1, k : k + 1]
        scale = jnp.where(first == k, lax.rsqrt(pivot), scale)
        if k < RANK - 1:
            ratio = work[:, k : k + 1] * (1.0 / pivot)
            work = jnp.where(below > k, work - ratio * top, work)
    out_ref[...] = pack(work[:, RANK:] * scale)


def inverse_factor(total, copies):
    return pl.pallas_call(
        functools.partial(factor_kernel, copies),
        in_specs=[pl.BlockSpec(memory_space=pltpu.VMEM)],
        out_specs=pl.BlockSpec(memory_space=pltpu.VMEM),
        out_shape=jax.ShapeDtypeStruct((8, LANES), F32),
        compiler_params=pltpu.CompilerParams(vmem_limit_bytes=VMEM_LIMIT),
        cost_estimate=pl.CostEstimate(flops=4_000_000, bytes_accessed=4_000_000, transcendentals=64),
        name="inverse_factor",
    )(total)


def piece_kernel(replicas, a_ref, b_ref, inverse_ref, out_ref):
    inverse = unpack(inverse_ref[...]) * (1.0 / replicas)
    q = dot(inverse, a_ref[...] + b_ref[...], ((1,), (0,)), lax.Precision.HIGHEST)
    both = jnp.concatenate([q, inverse_ref[...]], axis=0)
    out_ref[...] = jnp.broadcast_to(both[None], out_ref.shape)


def finished_piece(a, b, inverse, replicas, receivers):
    return pl.pallas_call(
        functools.partial(piece_kernel, replicas),
        in_specs=[pl.BlockSpec(memory_space=pltpu.VMEM)] * 3,
        out_specs=pl.BlockSpec(memory_space=pltpu.VMEM),
        out_shape=jax.ShapeDtypeStruct((receivers, RANK + 8, LANES), F32),
        compiler_params=pltpu.CompilerParams(vmem_limit_bytes=VMEM_LIMIT),
        name="finished_piece",
    )(a, b, inverse)


def update_kernel(replicas, place_ref, pieces_ref, p_ref, full_ref, m1_ref, m2_ref, err_ref, n1_ref, n2_ref, up_ref, q_ref, hat_ref, flat_ref):
    m, step = pl.program_id(0), pl.program_id(1)
    rows, width = err_ref.shape[2:]
    tiles = pieces_ref.shape[0]
    here = width // LANES

    @pl.when(step == 0)
    def _():
        inverse = unpack(pieces_ref[0, RANK:, :])
        p_hat = dot(inverse, p_ref[0] * (1.0 / replicas), ((1,), (0,)), lax.Precision.HIGHEST)
        hat = p_hat.T
        h_hi, h_lo = split(hat)
        hat_ref[...] = jnp.concatenate([h_hi, h_lo, h_hi], axis=1)
        mine = flat_ref.shape[0]
        at = lax.broadcasted_iota(jnp.int32, (8, rows), 0) + place_ref[0] * mine
        chosen = (lax.broadcasted_iota(jnp.int32, (8, rows), 1) == at).astype(F32)
        own = dot(chosen, hat, ((1,), (0,)), lax.Precision.HIGHEST)
        o_hi, o_lo = split(own)
        own3 = jnp.concatenate([o_hi, o_lo, o_hi], axis=1)
        q = jnp.concatenate([pieces_ref[j, :RANK, :] for j in range(tiles)], axis=1)
        q_ref[0] = q
        q_hi, q_lo = split(q)
        own_rows = dot(own3, jnp.concatenate([q_hi, q_hi, q_lo], axis=0), ((1,), (0,)))
        for j in range(tiles):
            flat_ref[:, j, :] = own_rows[:mine, j * LANES : (j + 1) * LANES]
        flat = flat_ref[...].reshape(mine * tiles, LANES)
        n1 = 0.9 * m1_ref[0] + 0.1 * flat
        n2 = 0.95 * m2_ref[0] + 0.05 * flat * flat
        n1_ref[0] = n1
        n2_ref[0] = n2
        up_ref[0] = (n1 / (jnp.sqrt(n2) + 1e-08)).astype(BF16)

    q = jnp.concatenate([pieces_ref[step * here + j, :RANK, :] for j in range(here)], axis=1)
    q_hi, q_lo = split(q)
    approx = dot(hat_ref[...], jnp.concatenate([q_hi, q_hi, q_lo], axis=0), ((1,), (0,)))
    err_ref[0, 0] = full_ref[m, :, pl.ds(pl.multiple_of(step * width, width), width)] - approx


def update(place, pieces, p_sum, full, moment1, moment2, replicas, blocks=2):
    projections, rows, columns = full.shape
    width, tiles = columns // blocks, columns // LANES
    state = moment1.shape[1]
    own = pl.BlockSpec((1, state, LANES), lambda m, k: (m, 0, 0))
    return pl.pallas_call(
        functools.partial(update_kernel, replicas),
        grid=(projections, blocks),
        in_specs=[
            pl.BlockSpec(memory_space=pltpu.SMEM),
            pl.BlockSpec((tiles, RANK + 8, LANES), lambda m, k: (m, 0, 0)),
            pl.BlockSpec((1, RANK, rows), lambda m, k: (m, 0, 0)),
            pl.BlockSpec(memory_space=pltpu.VMEM),
            own,
            own,
        ],
        out_specs=[
            pl.BlockSpec((1, 1, rows, width), lambda m, k: (0, m, 0, k)),
            own,
            own,
            own,
            pl.BlockSpec((1, RANK, columns), lambda m, k: (m, 0, 0)),
        ],
        out_shape=[
            jax.ShapeDtypeStruct((1, projections, rows, columns), F32),
            jax.ShapeDtypeStruct(moment1.shape, F32),
            jax.ShapeDtypeStruct(moment2.shape, F32),
            jax.ShapeDtypeStruct(moment1.shape, BF16),
            jax.ShapeDtypeStruct((projections, RANK, columns), F32),
        ],
        scratch_shapes=[
            pltpu.VMEM((rows, 3 * RANK), BF16),
            pltpu.VMEM((state // tiles, tiles, LANES), F32),
        ],
        compiler_params=pltpu.CompilerParams(vmem_limit_bytes=VMEM_LIMIT),
        name="update",
    )(place, pieces, p_sum, full, moment1, moment2)


def flip(axis, bit):
    return [(i, i ^ bit) for i in range(lax.axis_size(axis))]


def shards(grads, errors, q_prev, moment1, moment2):
    replicas = lax.axis_size(("z", "y"))
    full, p_sum = left_factors(grads, errors, q_prev)
    for axis, bit in (("y", 1), ("y", 2), ("z", 1), ("z", 2), ("z", 4)):
        p_sum = p_sum + lax.ppermute(p_sum, axis, flip(axis, bit))

    plane = ("y", "x", "c")
    owners = lax.axis_size(plane)
    terms = right_terms(p_sum, full, replicas)
    total = lax.all_to_all(terms, plane, 0, 0, tiled=True).sum(0)
    inverse = inverse_factor(total, lax.axis_size("y"))
    q = total[:RANK]
    q = q + lax.ppermute(q, "z", flip("z", 1))
    q = q + lax.ppermute(q, "z", flip("z", 2))
    piece = finished_piece(q, lax.ppermute(q, "z", flip("z", 4)), inverse, replicas, owners)
    pieces = lax.all_to_all(piece, plane, 0, 0, tiled=True)

    place = lax.axis_index(("z", "y"))[None]
    return tuple(update(place, pieces, p_sum, full, moment1, moment2, replicas))


def solution(mesh):
    mesh = Mesh(mesh.devices.reshape(8, 4, 4, 2), ("z", "y", "x", "c"))
    dp, fsdp = ("z", "y"), ("x", "c")
    blocks = P(dp, None, fsdp, None)
    states = P(None, fsdp + dp, None)
    return jax.shard_map(
        shards,
        mesh=mesh,
        in_specs=(blocks, blocks, P(), states, states),
        out_specs=(blocks, states, states, states, P()),
        check_vma=False,
    )
```

```python
import functools

import jax
import jax.numpy as jnp
from jax import lax
from jax.experimental import pallas as pl
from jax.experimental.pallas import tpu as pltpu
from jax.sharding import Mesh, PartitionSpec as P

F32 = jnp.float32
BF16 = jnp.bfloat16
RANK = 32
LANES = 128
VMEM_LIMIT = 24 * 2**20


def split(x):
    head = x.astype(BF16)
    return head, (x - head.astype(F32)).astype(BF16)


def in_hbm(x):
    return pltpu.with_memory_space_constraint(x, pltpu.HBM)


def dot(a, b, dims, precision=None):
    return lax.dot_general(a, b, (dims, ((), ())), precision=precision, preferred_element_type=F32)


def pack(square):
    return jnp.concatenate([square[8 * i : 8 * i + 8] for i in range(4)], axis=1)


def unpack(packed):
    return jnp.concatenate([packed[:, 32 * i : 32 * i + 32] for i in range(4)], axis=0)


def left_kernel(grads_ref, errors_ref, q_ref, full_ref, p_ref):
    m, step = pl.program_id(0), pl.program_id(1)
    full = grads_ref[0, 0].astype(F32) + errors_ref[0, 0]
    width = full.shape[1]
    full_ref[m, :, pl.ds(pl.multiple_of(step * width, width), width)] = full
    f_hi, f_lo = split(full)
    q_hi, q_lo = split(q_ref[0])
    wide = dot(jnp.concatenate([q_hi, q_lo], axis=0), f_hi, ((1,), (1,)))
    part = wide[:RANK] + wide[RANK:] + dot(q_hi, f_lo, ((1,), (1,)))

    @pl.when(step == 0)
    def _():
        p_ref[0] = part

    @pl.when(step > 0)
    def _():
        p_ref[0] += part


def left_factors(grads, errors, q_prev, blocks=2):
    _, projections, rows, columns = grads.shape
    width = columns // blocks
    return pl.pallas_call(
        left_kernel,
        grid=(projections, blocks),
        in_specs=[
            pl.BlockSpec((1, 1, rows, width), lambda m, k: (0, m, 0, k)),
            pl.BlockSpec((1, 1, rows, width), lambda m, k: (0, m, 0, k)),
            pl.BlockSpec((1, RANK, width), lambda m, k: (m, 0, k)),
        ],
        out_specs=[
            pl.BlockSpec(memory_space=pltpu.VMEM),
            pl.BlockSpec((1, RANK, rows), lambda m, k: (m, 0, 0)),
        ],
        out_shape=[
            pltpu.VMEM((projections, rows, columns), F32),
            jax.ShapeDtypeStruct((projections, RANK, rows), F32),
        ],
        compiler_params=pltpu.CompilerParams(vmem_limit_bytes=VMEM_LIMIT),
        name="left_factors",
    )(in_hbm(grads), in_hbm(errors), in_hbm(q_prev))


def right_kernel(replicas, place_ref, p_ref, full_ref, keep_ref, send_ref):
    slots, height, _ = keep_ref.shape
    tiles = (height - 8) // RANK
    width = tiles * LANES
    x, core = place_ref[1], place_ref[2]
    for out_ref, m in ((send_ref, 1 - core), (keep_ref, core)):
        p = p_ref[m] * (1.0 / replicas)
        p_hi, p_lo = split(p)
        both = jnp.concatenate([p_hi, p_lo], axis=0)
        gram = pack(dot(p, p, ((1,), (1,)), lax.Precision.HIGHEST))
        for slot in range(slots):
            first = pl.multiple_of((x ^ slot) * width, width)
            f_hi, f_lo = split(full_ref[m, :, pl.ds(first, width)])
            wide = dot(both, f_hi, ((1,), (0,)))
            q = wide[:RANK] + wide[RANK:] + dot(p_hi, f_lo, ((1,), (0,)))
            for j in range(tiles):
                out_ref[slot, j * RANK : (j + 1) * RANK, :] = q[:, j * LANES : (j + 1) * LANES]
            out_ref[slot, tiles * RANK :, :] = gram


def right_terms(place, p_sum, full, replicas, slots):
    columns = full.shape[2]
    piece = jax.ShapeDtypeStruct((slots, columns // slots // LANES * RANK + 8, LANES), F32)
    return pl.pallas_call(
        functools.partial(right_kernel, replicas),
        in_specs=[pl.BlockSpec(memory_space=pltpu.SMEM)] + [pl.BlockSpec(memory_space=pltpu.VMEM)] * 2,
        out_specs=[pl.BlockSpec(memory_space=pltpu.VMEM)] * 2,
        out_shape=[piece, piece],
        compiler_params=pltpu.CompilerParams(vmem_limit_bytes=VMEM_LIMIT),
        name="right_terms",
    )(place, p_sum, full)


def factor_kernel(sum_ref, out_ref):
    gram = unpack(sum_ref[sum_ref.shape[0] - 8 :, :])
    row = lax.broadcasted_iota(jnp.int32, (RANK, RANK), 0)
    column = lax.broadcasted_iota(jnp.int32, (RANK, RANK), 1)
    work = jnp.concatenate([gram, (row == column).astype(F32)], axis=1)
    below = lax.broadcasted_iota(jnp.int32, (RANK, 2 * RANK), 0)
    scale = jnp.zeros((RANK, 1), F32)
    first = lax.broadcasted_iota(jnp.int32, (RANK, 1), 0)
    for k in range(RANK):
        top = work[k : k + 1, :]
        pivot = work[k : k + 1, k : k + 1]
        scale = jnp.where(first == k, lax.rsqrt(pivot), scale)
        if k < RANK - 1:
            ratio = work[:, k : k + 1] * (1.0 / pivot)
            work = jnp.where(below > k, work - ratio * top, work)
    out_ref[...] = pack(work[:, RANK:] * scale)


def inverse_factor(total):
    return pl.pallas_call(
        factor_kernel,
        in_specs=[pl.BlockSpec(memory_space=pltpu.VMEM)],
        out_specs=pl.BlockSpec(memory_space=pltpu.VMEM),
        out_shape=jax.ShapeDtypeStruct((8, LANES), F32),
        compiler_params=pltpu.CompilerParams(vmem_limit_bytes=VMEM_LIMIT),
        cost_estimate=pl.CostEstimate(flops=4_000_000, bytes_accessed=4_000_000, transcendentals=64),
        name="inverse_factor",
    )(total)


def piece_kernel(replicas, a_ref, b_ref, inverse_ref, out_ref):
    inverse = unpack(inverse_ref[...]) * (1.0 / replicas)
    tiles = a_ref.shape[0] // RANK
    rows = a_ref[...] + b_ref[...]
    wide = jnp.concatenate([rows[j * RANK : (j + 1) * RANK] for j in range(tiles)], axis=1)
    q = dot(inverse, wide, ((1,), (0,)), lax.Precision.HIGHEST)
    for j in range(tiles):
        out_ref[j * RANK : (j + 1) * RANK, :] = q[:, j * LANES : (j + 1) * LANES]
    out_ref[tiles * RANK :, :] = inverse_ref[...]


def finished_piece(a, b, inverse, replicas):
    return pl.pallas_call(
        functools.partial(piece_kernel, replicas),
        in_specs=[pl.BlockSpec(memory_space=pltpu.VMEM)] * 3,
        out_specs=pl.BlockSpec(memory_space=pltpu.VMEM),
        out_shape=jax.ShapeDtypeStruct((a.shape[0] + 8, LANES), F32),
        compiler_params=pltpu.CompilerParams(vmem_limit_bytes=VMEM_LIMIT),
        name="finished_piece",
    )(a, b, inverse)


def update_kernel(replicas, place_ref, own_ref, other_ref, p_ref, full_ref, m1_ref, m2_ref, err_ref, n1_ref, n2_ref, up_ref, q_ref, hat_ref, flat_ref):
    m, step = pl.program_id(0), pl.program_id(1)
    rows, width = err_ref.shape[2:]
    slots, height, _ = own_ref.shape
    tiles = (height - 8) // RANK
    x, mine_here = place_ref[1], m == place_ref[2]

    def piece(block):
        return jnp.where(mine_here, own_ref[block ^ x], other_ref[block ^ x])

    def wide(block):
        rows_of = piece(block)
        return [rows_of[j * RANK : (j + 1) * RANK] for j in range(tiles)]

    @pl.when(step == 0)
    def _():
        inverse = unpack(piece(0)[tiles * RANK :])
        p_hat = dot(inverse, p_ref[0] * (1.0 / replicas), ((1,), (0,)), lax.Precision.HIGHEST)
        hat = p_hat.T
        h_hi, h_lo = split(hat)
        hat_ref[...] = jnp.concatenate([h_hi, h_lo, h_hi], axis=1)
        mine = flat_ref.shape[0]
        at = lax.broadcasted_iota(jnp.int32, (8, rows), 0) + place_ref[0] * mine
        chosen = (lax.broadcasted_iota(jnp.int32, (8, rows), 1) == at).astype(F32)
        own = dot(chosen, hat, ((1,), (0,)), lax.Precision.HIGHEST)
        o_hi, o_lo = split(own)
        own3 = jnp.concatenate([o_hi, o_lo, o_hi], axis=1)
        q = jnp.concatenate([t for block in range(slots) for t in wide(block)], axis=1)
        q_ref[0] = q
        q_hi, q_lo = split(q)
        own_rows = dot(own3, jnp.concatenate([q_hi, q_hi, q_lo], axis=0), ((1,), (0,)))
        for j in range(slots * tiles):
            flat_ref[:, j, :] = own_rows[:mine, j * LANES : (j + 1) * LANES]
        flat = flat_ref[...].reshape(mine * slots * tiles, LANES)
        n1 = 0.9 * m1_ref[0] + 0.1 * flat
        n2 = 0.95 * m2_ref[0] + 0.05 * flat * flat
        n1_ref[0] = n1
        n2_ref[0] = n2
        up_ref[0] = (n1 / (jnp.sqrt(n2) + 1e-08)).astype(BF16)

    here = width // LANES // tiles
    q = jnp.concatenate([t for j in range(here) for t in wide(step * here + j)], axis=1)
    q_hi, q_lo = split(q)
    approx = dot(hat_ref[...], jnp.concatenate([q_hi, q_hi, q_lo], axis=0), ((1,), (0,)))
    err_ref[0, 0] = full_ref[m, :, pl.ds(pl.multiple_of(step * width, width), width)] - approx


def update(place, own, other, p_sum, full, moment1, moment2, replicas, blocks=2):
    projections, rows, columns = full.shape
    width, tiles = columns // blocks, columns // LANES
    state = moment1.shape[1]
    states = pl.BlockSpec((1, state, LANES), lambda m, k: (m, 0, 0))
    return pl.pallas_call(
        functools.partial(update_kernel, replicas),
        grid=(projections, blocks),
        in_specs=[
            pl.BlockSpec(memory_space=pltpu.SMEM),
            pl.BlockSpec(memory_space=pltpu.VMEM),
            pl.BlockSpec(memory_space=pltpu.VMEM),
            pl.BlockSpec((1, RANK, rows), lambda m, k: (m, 0, 0)),
            pl.BlockSpec(memory_space=pltpu.VMEM),
            states,
            states,
        ],
        out_specs=[
            pl.BlockSpec((1, 1, rows, width), lambda m, k: (0, m, 0, k)),
            states,
            states,
            states,
            pl.BlockSpec((1, RANK, columns), lambda m, k: (m, 0, 0)),
        ],
        out_shape=[
            jax.ShapeDtypeStruct((1, projections, rows, columns), F32),
            jax.ShapeDtypeStruct(moment1.shape, F32),
            jax.ShapeDtypeStruct(moment2.shape, F32),
            jax.ShapeDtypeStruct(moment1.shape, BF16),
            jax.ShapeDtypeStruct((projections, RANK, columns), F32),
        ],
        scratch_shapes=[
            pltpu.VMEM((rows, 3 * RANK), BF16),
            pltpu.VMEM((state // tiles, tiles, LANES), F32),
        ],
        compiler_params=pltpu.CompilerParams(vmem_limit_bytes=VMEM_LIMIT),
        name="update",
    )(place, own, other, p_sum, full, moment1, moment2)


def swap(value, axis, bit):
    return lax.ppermute(value, axis, [(i, i ^ bit) for i in range(lax.axis_size(axis))])


def four(values, axis):
    return (values[0] + swap(values[1], axis, 1)) + (swap(values[2], axis, 2) + swap(values[3], axis, 3))


def sum_replicas(value):
    value = four([value] * 4, "y")
    value = four([value] * 4, "z")
    return value, swap(value, "z", 4)


def shards(grads, errors, q_prev, moment1, moment2):
    replicas, slots = lax.axis_size(("z", "y")), lax.axis_size("x")
    place = jnp.stack([lax.axis_index(("z", "y")), lax.axis_index("x"), lax.axis_index("c")])
    full, p_local = left_factors(grads, errors, q_prev)
    p_low, p_high = sum_replicas(p_local)
    p_sum = p_low + p_high

    keep, send = right_terms(place, p_sum, full, replicas, slots)
    terms = keep + swap(send, "c", 1)
    total = four([terms[i] for i in range(slots)], "x")
    inverse = inverse_factor(total)
    piece = finished_piece(*sum_replicas(total[:-8]), inverse, replicas)
    own = jnp.stack([piece] + [swap(piece, "x", i) for i in range(1, slots)])
    other = swap(own, "c", 1)
    return tuple(update(place, own, other, p_sum, full, moment1, moment2, replicas))


def solution(mesh):
    mesh = Mesh(mesh.devices.reshape(8, 4, 4, 2), ("z", "y", "x", "c"))
    dp, fsdp = ("z", "y"), ("x", "c")
    blocks = P(dp, None, fsdp, None)
    states = P(None, fsdp + dp, None)
    return jax.shard_map(
        shards,
        mesh=mesh,
        in_specs=(blocks, blocks, P(), states, states),
        out_specs=(blocks, states, states, states, P()),
        check_vma=False,
    )
```

```python
import functools

import jax
import jax.numpy as jnp
from jax import lax
from jax.experimental import pallas as pl
from jax.experimental.pallas import tpu as pltpu
from jax.sharding import Mesh, PartitionSpec as P

F32 = jnp.float32
BF16 = jnp.bfloat16
RANK = 32
LANES = 128
VMEM_LIMIT = 24 * 2**20


def split(x):
    head = x.astype(BF16)
    return head, (x - head.astype(F32)).astype(BF16)


def in_hbm(x):
    return pltpu.with_memory_space_constraint(x, pltpu.HBM)


def dot(a, b, dims, precision=None):
    return lax.dot_general(a, b, (dims, ((), ())), precision=precision, preferred_element_type=F32)


def pack(square):
    return jnp.concatenate([square[8 * i : 8 * i + 8] for i in range(4)], axis=1)


def unpack(packed):
    return jnp.concatenate([packed[:, 32 * i : 32 * i + 32] for i in range(4)], axis=0)


def left_kernel(grads_ref, errors_ref, q_ref, full_ref, p_ref):
    m, step = pl.program_id(0), pl.program_id(1)
    full = grads_ref[0, 0].astype(F32) + errors_ref[0, 0]
    width = full.shape[1]
    full_ref[m, :, pl.ds(pl.multiple_of(step * width, width), width)] = full
    f_hi, f_lo = split(full)
    q_hi, q_lo = split(q_ref[0])
    wide = dot(jnp.concatenate([q_hi, q_lo], axis=0), f_hi, ((1,), (1,)))
    part = wide[:RANK] + wide[RANK:] + dot(q_hi, f_lo, ((1,), (1,)))

    @pl.when(step == 0)
    def _():
        p_ref[0] = part

    @pl.when(step > 0)
    def _():
        p_ref[0] += part


def left_factors(grads, errors, q_prev, blocks=2):
    _, projections, rows, columns = grads.shape
    width = columns // blocks
    return pl.pallas_call(
        left_kernel,
        grid=(projections, blocks),
        in_specs=[
            pl.BlockSpec((1, 1, rows, width), lambda m, k: (0, m, 0, k)),
            pl.BlockSpec((1, 1, rows, width), lambda m, k: (0, m, 0, k)),
            pl.BlockSpec((1, RANK, width), lambda m, k: (m, 0, k)),
        ],
        out_specs=[
            pl.BlockSpec(memory_space=pltpu.VMEM),
            pl.BlockSpec((1, RANK, rows), lambda m, k: (m, 0, 0)),
        ],
        out_shape=[
            pltpu.VMEM((projections, rows, columns), F32),
            jax.ShapeDtypeStruct((projections, RANK, rows), F32),
        ],
        compiler_params=pltpu.CompilerParams(vmem_limit_bytes=VMEM_LIMIT),
        name="left_factors",
    )(in_hbm(grads), in_hbm(errors), in_hbm(q_prev))


def right_kernel(replicas, p_ref, full_ref, keep_ref, send_ref):
    slots, height, _ = keep_ref.shape
    tiles = (height - 8) // RANK
    width = tiles * LANES
    x, core = lax.axis_index("x"), lax.axis_index("c")
    for out_ref, m in ((send_ref, 1 - core), (keep_ref, core)):
        p = p_ref[m] * (1.0 / replicas)
        p_hi, p_lo = split(p)
        both = jnp.concatenate([p_hi, p_lo], axis=0)
        gram = pack(dot(p, p, ((1,), (1,)), lax.Precision.HIGHEST))
        for slot in range(slots):
            first = pl.multiple_of((x ^ slot) * width, width)
            f_hi, f_lo = split(full_ref[m, :, pl.ds(first, width)])
            wide = dot(both, f_hi, ((1,), (0,)))
            q = wide[:RANK] + wide[RANK:] + dot(p_hi, f_lo, ((1,), (0,)))
            for j in range(tiles):
                out_ref[slot, j * RANK : (j + 1) * RANK, :] = q[:, j * LANES : (j + 1) * LANES]
            out_ref[slot, tiles * RANK :, :] = gram


def right_terms(p_sum, full, replicas, slots):
    columns = full.shape[2]
    piece = jax.ShapeDtypeStruct((slots, columns // slots // LANES * RANK + 8, LANES), F32)
    return pl.pallas_call(
        functools.partial(right_kernel, replicas),
        in_specs=[pl.BlockSpec(memory_space=pltpu.VMEM)] * 2,
        out_specs=[pl.BlockSpec(memory_space=pltpu.VMEM)] * 2,
        out_shape=[piece, piece],
        compiler_params=pltpu.CompilerParams(vmem_limit_bytes=VMEM_LIMIT),
        name="right_terms",
    )(p_sum, full)


def factor_kernel(sum_ref, out_ref):
    gram = unpack(sum_ref[sum_ref.shape[0] - 8 :, :])
    row = lax.broadcasted_iota(jnp.int32, (RANK, RANK), 0)
    column = lax.broadcasted_iota(jnp.int32, (RANK, RANK), 1)
    work = jnp.concatenate([gram, (row == column).astype(F32)], axis=1)
    below = lax.broadcasted_iota(jnp.int32, (RANK, 2 * RANK), 0)
    scale = jnp.zeros((RANK, 1), F32)
    first = lax.broadcasted_iota(jnp.int32, (RANK, 1), 0)
    for k in range(RANK):
        top = work[k : k + 1, :]
        pivot = work[k : k + 1, k : k + 1]
        scale = jnp.where(first == k, lax.rsqrt(pivot), scale)
        if k < RANK - 1:
            ratio = work[:, k : k + 1] * (1.0 / pivot)
            work = jnp.where(below > k, work - ratio * top, work)
    out_ref[...] = pack(work[:, RANK:] * scale)


def inverse_factor(total):
    return pl.pallas_call(
        factor_kernel,
        in_specs=[pl.BlockSpec(memory_space=pltpu.VMEM)],
        out_specs=pl.BlockSpec(memory_space=pltpu.VMEM),
        out_shape=jax.ShapeDtypeStruct((8, LANES), F32),
        compiler_params=pltpu.CompilerParams(vmem_limit_bytes=VMEM_LIMIT),
        cost_estimate=pl.CostEstimate(flops=4_000_000, bytes_accessed=4_000_000, transcendentals=64),
        name="inverse_factor",
    )(total)


def piece_kernel(replicas, a_ref, b_ref, inverse_ref, out_ref):
    inverse = unpack(inverse_ref[...]) * (1.0 / replicas)
    tiles = a_ref.shape[0] // RANK
    rows = a_ref[...] + b_ref[...]
    wide = jnp.concatenate([rows[j * RANK : (j + 1) * RANK] for j in range(tiles)], axis=1)
    q = dot(inverse, wide, ((1,), (0,)), lax.Precision.HIGHEST)
    for j in range(tiles):
        out_ref[j * RANK : (j + 1) * RANK, :] = q[:, j * LANES : (j + 1) * LANES]
    out_ref[tiles * RANK :, :] = inverse_ref[...]


def finished_piece(a, b, inverse, replicas):
    return pl.pallas_call(
        functools.partial(piece_kernel, replicas),
        in_specs=[pl.BlockSpec(memory_space=pltpu.VMEM)] * 3,
        out_specs=pl.BlockSpec(memory_space=pltpu.VMEM),
        out_shape=jax.ShapeDtypeStruct((a.shape[0] + 8, LANES), F32),
        compiler_params=pltpu.CompilerParams(vmem_limit_bytes=VMEM_LIMIT),
        name="finished_piece",
    )(a, b, inverse)


def update_kernel(replicas, own_ref, other_ref, p_ref, full_ref, m1_ref, m2_ref, err_ref, n1_ref, n2_ref, up_ref, q_ref, hat_ref, flat_ref):
    m, step = pl.program_id(0), pl.program_id(1)
    rows, width = err_ref.shape[2:]
    slots, height, _ = own_ref.shape
    tiles = (height - 8) // RANK
    x, mine_here = lax.axis_index("x"), m == lax.axis_index("c")

    def piece(block):
        return jnp.where(mine_here, own_ref[block ^ x], other_ref[block ^ x])

    def wide(block):
        rows_of = piece(block)
        return [rows_of[j * RANK : (j + 1) * RANK] for j in range(tiles)]

    @pl.when(step == 0)
    def _():
        inverse = unpack(piece(0)[tiles * RANK :])
        p_hat = dot(inverse, p_ref[0] * (1.0 / replicas), ((1,), (0,)), lax.Precision.HIGHEST)
        hat = p_hat.T
        h_hi, h_lo = split(hat)
        hat_ref[...] = jnp.concatenate([h_hi, h_lo, h_hi], axis=1)
        mine = flat_ref.shape[0]
        at = lax.broadcasted_iota(jnp.int32, (8, rows), 0) + lax.axis_index(("z", "y")) * mine
        chosen = (lax.broadcasted_iota(jnp.int32, (8, rows), 1) == at).astype(F32)
        own = dot(chosen, hat, ((1,), (0,)), lax.Precision.HIGHEST)
        o_hi, o_lo = split(own)
        own3 = jnp.concatenate([o_hi, o_lo, o_hi], axis=1)
        q = jnp.concatenate([t for block in range(slots) for t in wide(block)], axis=1)
        q_ref[0] = q
        q_hi, q_lo = split(q)
        own_rows = dot(own3, jnp.concatenate([q_hi, q_hi, q_lo], axis=0), ((1,), (0,)))
        for j in range(slots * tiles):
            flat_ref[:, j, :] = own_rows[:mine, j * LANES : (j + 1) * LANES]
        flat = flat_ref[...].reshape(mine * slots * tiles, LANES)
        n1 = 0.9 * m1_ref[0] + 0.1 * flat
        n2 = 0.95 * m2_ref[0] + 0.05 * flat * flat
        n1_ref[0] = n1
        n2_ref[0] = n2
        up_ref[0] = (n1 / (jnp.sqrt(n2) + 1e-08)).astype(BF16)

    here = width // LANES // tiles
    q = jnp.concatenate([t for j in range(here) for t in wide(step * here + j)], axis=1)
    q_hi, q_lo = split(q)
    approx = dot(hat_ref[...], jnp.concatenate([q_hi, q_hi, q_lo], axis=0), ((1,), (0,)))
    err_ref[0, 0] = full_ref[m, :, pl.ds(pl.multiple_of(step * width, width), width)] - approx


def update(own, other, p_sum, full, moment1, moment2, replicas, blocks=2):
    projections, rows, columns = full.shape
    width, tiles = columns // blocks, columns // LANES
    state = moment1.shape[1]
    states = pl.BlockSpec((1, state, LANES), lambda m, k: (m, 0, 0))
    return pl.pallas_call(
        functools.partial(update_kernel, replicas),
        grid=(projections, blocks),
        in_specs=[
            pl.BlockSpec(memory_space=pltpu.VMEM),
            pl.BlockSpec(memory_space=pltpu.VMEM),
            pl.BlockSpec((1, RANK, rows), lambda m, k: (m, 0, 0)),
            pl.BlockSpec(memory_space=pltpu.VMEM),
            states,
            states,
        ],
        out_specs=[
            pl.BlockSpec((1, 1, rows, width), lambda m, k: (0, m, 0, k)),
            states,
            states,
            states,
            pl.BlockSpec((1, RANK, columns), lambda m, k: (m, 0, 0)),
        ],
        out_shape=[
            jax.ShapeDtypeStruct((1, projections, rows, columns), F32),
            jax.ShapeDtypeStruct(moment1.shape, F32),
            jax.ShapeDtypeStruct(moment2.shape, F32),
            jax.ShapeDtypeStruct(moment1.shape, BF16),
            jax.ShapeDtypeStruct((projections, RANK, columns), F32),
        ],
        scratch_shapes=[
            pltpu.VMEM((rows, 3 * RANK), BF16),
            pltpu.VMEM((state // tiles, tiles, LANES), F32),
        ],
        compiler_params=pltpu.CompilerParams(vmem_limit_bytes=VMEM_LIMIT),
        name="update",
    )(own, other, p_sum, full, moment1, moment2)


def swap(value, axis, bit):
    return lax.ppermute(value, axis, [(i, i ^ bit) for i in range(lax.axis_size(axis))])


def four(values, axis):
    return (values[0] + swap(values[1], axis, 1)) + (swap(values[2], axis, 2) + swap(values[3], axis, 3))


def sum_replicas(value, other=None):
    value = four([value] * 4, "y")
    if other is not None:
        value, other = lax.optimization_barrier((value, other))
    value = four([value] * 4, "z")
    return value, swap(value, "z", 6), other


def shards(grads, errors, q_prev, moment1, moment2):
    replicas, slots = lax.axis_size(("z", "y")), lax.axis_size("x")
    full, p_local = left_factors(grads, errors, q_prev)
    p_low, p_high, _ = sum_replicas(p_local)
    p_sum = p_low + p_high

    keep, send = right_terms(p_sum, full, replicas, slots)
    terms = keep + swap(send, "c", 1)
    total = four([terms[i] for i in range(slots)], "x")
    piece = finished_piece(*sum_replicas(total[:-8], inverse_factor(total)), replicas)
    own = jnp.stack([piece] + [swap(piece, "x", i) for i in range(1, slots)])
    other = swap(own, "c", 1)
    return tuple(update(own, other, p_sum, full, moment1, moment2, replicas))


def solution(mesh):
    mesh = Mesh(mesh.devices.reshape(8, 4, 4, 2), ("z", "y", "x", "c"))
    dp, fsdp = ("z", "y"), ("x", "c")
    blocks = P(dp, None, fsdp, None)
    states = P(None, fsdp + dp, None)
    return jax.shard_map(
        shards,
        mesh=mesh,
        in_specs=(blocks, blocks, P(), states, states),
        out_specs=(blocks, states, states, states, P()),
        check_vma=False,
    )
```

```python
import functools

import jax
import jax.numpy as jnp
from jax import lax
from jax.experimental import pallas as pl
from jax.experimental.pallas import tpu as pltpu
from jax.sharding import Mesh, PartitionSpec as P

F32 = jnp.float32
BF16 = jnp.bfloat16
RANK = 32
LANES = 128
VMEM_LIMIT = 24 * 2**20
PARAMS = pltpu.CompilerParams(vmem_limit_bytes=VMEM_LIMIT)
WHOLE = pl.BlockSpec(memory_space=pltpu.VMEM)
AWAY = pl.BlockSpec(memory_space=pl.ANY)


def in_hbm(x):
    return pltpu.with_memory_space_constraint(x, pltpu.HBM)


def split(x):
    head = x.astype(BF16)
    return head, (x - head.astype(F32)).astype(BF16)


def left_three(x):
    hi, lo = split(x)
    return jnp.concatenate([hi, lo, hi], axis=1)


def right_three(x):
    hi, lo = split(x)
    return jnp.concatenate([hi, hi, lo], axis=0)


def dot(a, b, a_dim, b_dim, precision=None):
    return lax.dot_general(a, b, (((a_dim,), (b_dim,)), ((), ())), precision=precision, preferred_element_type=F32)


def pack(square):
    return jnp.concatenate([square[8 * i : 8 * i + 8] for i in range(4)], axis=1)


def unpack(packed):
    return jnp.concatenate([packed[:, 32 * i : 32 * i + 32] for i in range(4)], axis=0)


def left_columns(packed, m):
    columns = [packed[:, RANK * i : RANK * i + RANK] for i in range(4)]
    return jnp.concatenate([jnp.where(m == 0, columns[0], columns[1]), jnp.where(m == 0, columns[2], columns[3])], axis=0)


def left_kernel(grads_hbm, errors_hbm, q_hbm, full_ref, p_ref, grads_ref, q_ref, grads_sem, errors_sem, q_sem):
    projections, rows, _ = full_ref.shape
    q_copy = pltpu.make_async_copy(q_hbm, q_ref, q_sem)
    copies = [
        (
            pltpu.make_async_copy(grads_hbm.at[0, m], grads_ref.at[m], grads_sem.at[m]),
            pltpu.make_async_copy(errors_hbm.at[0, m], full_ref.at[m], errors_sem.at[m]),
        )
        for m in range(projections)
    ]
    q_copy.start()
    for pair in copies:
        for copy in pair:
            copy.start()
    q_copy.wait()
    for m, pair in enumerate(copies):
        q_hi, q_lo = split(q_ref[m])
        both = jnp.concatenate([q_hi, q_lo], axis=0)
        for copy in pair:
            copy.wait()
        full = grads_ref[m].astype(F32) + full_ref[m]
        full_ref[m] = full
        f_hi, f_lo = split(full)
        wide = dot(f_hi, both, 1, 1)
        p = wide[:, :RANK] + wide[:, RANK:] + dot(f_lo, q_hi, 1, 1)
        p_ref[:, RANK * m : RANK * (m + 1)] = p[: rows // 2]
        p_ref[:, RANK * (2 + m) : RANK * (3 + m)] = p[rows // 2 :]


def left_factors(grads, errors, q_prev):
    _, projections, rows, columns = grads.shape
    return pl.pallas_call(
        left_kernel,
        in_specs=[AWAY] * 3,
        out_specs=[WHOLE] * 2,
        out_shape=[pltpu.VMEM((projections, rows, columns), F32), pltpu.VMEM((rows // 2, LANES), F32)],
        scratch_shapes=[
            pltpu.VMEM((projections, rows, columns), BF16),
            pltpu.VMEM(q_prev.shape, F32),
            pltpu.SemaphoreType.DMA((projections,)),
            pltpu.SemaphoreType.DMA((projections,)),
            pltpu.SemaphoreType.DMA,
        ],
        compiler_params=PARAMS,
        name="left_factors",
    )(in_hbm(grads), in_hbm(errors), in_hbm(q_prev))


def right_kernel(replicas, mine, p_ref, full_ref, out_ref):
    slots, height, _ = out_ref.shape
    tiles = (height - 8) // RANK
    width = tiles * LANES
    x, core = lax.axis_index("x"), lax.axis_index("c")
    m = core if mine else 1 - core
    p = (left_columns(p_ref[...], m) * (1.0 / replicas)).T
    p_hi, p_lo = split(p)
    both = jnp.concatenate([p_hi, p_lo], axis=0)
    gram = pack(dot(p, p, 1, 1, lax.Precision.HIGHEST))
    for slot in range(slots):
        first = pl.multiple_of((x ^ slot) * width, width)
        f_hi, f_lo = split(full_ref[m, :, pl.ds(first, width)])
        wide = dot(both, f_hi, 1, 0)
        q = wide[:RANK] + wide[RANK:] + dot(p_hi, f_lo, 1, 0)
        for j in range(tiles):
            out_ref[slot, j * RANK : (j + 1) * RANK, :] = q[:, j * LANES : (j + 1) * LANES]
        out_ref[slot, tiles * RANK :, :] = gram


def right_terms(p_sum, full, replicas, slots, mine):
    height = full.shape[2] // slots // LANES * RANK + 8
    return pl.pallas_call(
        functools.partial(right_kernel, replicas, mine),
        in_specs=[WHOLE] * 2,
        out_specs=WHOLE,
        out_shape=jax.ShapeDtypeStruct((slots, height, LANES), F32),
        compiler_params=PARAMS,
        name="right_terms_own" if mine else "right_terms_other",
    )(p_sum, full)


def factor_kernel(sum_ref, out_ref):
    gram = unpack(sum_ref[sum_ref.shape[0] - 8 :, :])
    row = lax.broadcasted_iota(jnp.int32, (RANK, RANK), 0)
    column = lax.broadcasted_iota(jnp.int32, (RANK, RANK), 1)
    work = jnp.concatenate([gram, (row == column).astype(F32)], axis=1)
    below = lax.broadcasted_iota(jnp.int32, (RANK, 2 * RANK), 0)
    scale = jnp.zeros((RANK, 1), F32)
    first = lax.broadcasted_iota(jnp.int32, (RANK, 1), 0)
    for k in range(RANK):
        top = work[k : k + 1, :]
        pivot = work[k : k + 1, k : k + 1]
        scale = jnp.where(first == k, lax.rsqrt(pivot), scale)
        if k < RANK - 1:
            ratio = work[:, k : k + 1] * (1.0 / pivot)
            work = jnp.where(below > k, work - ratio * top, work)
    out_ref[...] = pack(work[:, RANK:] * scale)


def inverse_factor(total):
    return pl.pallas_call(
        factor_kernel,
        in_specs=[WHOLE],
        out_specs=WHOLE,
        out_shape=jax.ShapeDtypeStruct((8, LANES), F32),
        compiler_params=PARAMS,
        cost_estimate=pl.CostEstimate(flops=4_000_000, bytes_accessed=4_000_000, transcendentals=64),
        name="inverse_factor",
    )(total)


def hat_kernel(replicas, p_ref, own_ref, other_ref, hat_ref, rows_ref):
    rows = hat_ref.shape[1]
    share = rows // replicas
    core = lax.axis_index("c")
    at = lax.broadcasted_iota(jnp.int32, (16, rows), 0) + lax.axis_index(("z", "y")) * share
    chosen = (lax.broadcasted_iota(jnp.int32, (16, rows), 1) == at).astype(F32)
    for i, (inverse_ref, m) in enumerate(((own_ref, core), (other_ref, 1 - core))):
        p = left_columns(p_ref[...], m) * (1.0 / replicas)
        hat = dot(p, unpack(inverse_ref[...]), 1, 1, lax.Precision.HIGHEST)
        hat_ref[i] = left_three(hat)
        rows_ref[i] = left_three(dot(chosen, hat, 1, 0, lax.Precision.HIGHEST))


def orthonormal(p_sum, own, other, replicas):
    rows = 2 * p_sum.shape[0]
    return pl.pallas_call(
        functools.partial(hat_kernel, replicas),
        in_specs=[WHOLE] * 3,
        out_specs=[WHOLE] * 2,
        out_shape=[jax.ShapeDtypeStruct((2, rows, 3 * RANK), BF16), jax.ShapeDtypeStruct((2, 16, 3 * RANK), BF16)],
        compiler_params=PARAMS,
        cost_estimate=pl.CostEstimate(flops=4_000_000, bytes_accessed=3_000_000, transcendentals=64),
        name="orthonormal",
    )(p_sum, own, other)


def piece_kernel(replicas, a_ref, b_ref, inverse_ref, out_ref):
    inverse = unpack(inverse_ref[...]) * (1.0 / replicas)
    tiles = a_ref.shape[0] // RANK
    rows = a_ref[...] + b_ref[...]
    wide = jnp.concatenate([rows[j * RANK : (j + 1) * RANK] for j in range(tiles)], axis=1)
    q = dot(inverse, wide, 1, 0, lax.Precision.HIGHEST)
    for j in range(tiles):
        out_ref[j * RANK : (j + 1) * RANK, :] = q[:, j * LANES : (j + 1) * LANES]


def finished_piece(a, b, inverse, replicas):
    return pl.pallas_call(
        functools.partial(piece_kernel, replicas),
        in_specs=[WHOLE] * 3,
        out_specs=WHOLE,
        out_shape=jax.ShapeDtypeStruct(a.shape, F32),
        compiler_params=PARAMS,
        name="finished_piece",
    )(a, b, inverse)


def update_kernel(mine, pieces_ref, hat_ref, rows_ref, full_ref, m1_ref, m2_ref, *refs):
    err_hbm, n1_hbm, n2_hbm, up_hbm, q_hbm, err_ref, n1_ref, n2_ref, up_ref, q_ref, tile_ref, flat_ref, err_sem, sem = refs[-14:]
    slots, height, _ = pieces_ref.shape
    tiles = height // RANK
    width = tiles * LANES
    x, core = lax.axis_index("x"), lax.axis_index("c")
    i, m = (0, core) if mine else (1, 1 - core)
    copies = []
    for slot in range(slots):
        block = x ^ slot
        here = pl.ds(pl.multiple_of(block * width, width), width)
        q = jnp.concatenate([pieces_ref[slot, j * RANK : (j + 1) * RANK, :] for j in range(tiles)], axis=1)
        right = right_three(q)
        err_ref[slot] = full_ref[m, :, here] - dot(hat_ref[i], right, 1, 0)
        copies.append(pltpu.make_async_copy(err_ref.at[slot], err_hbm.at[0, m, :, here], err_sem.at[slot]))
        copies[-1].start()
        q_ref[:, here] = q
        state = dot(rows_ref[i], right, 1, 0)
        for j in range(tiles):
            tile_ref[block * tiles + j] = state[:8, j * LANES : (j + 1) * LANES]
    share = flat_ref.shape[0]
    for j in range(slots * tiles):
        flat_ref[:, j, :] = tile_ref[j, :share, :]
    flat = flat_ref[...].reshape(share * slots * tiles, LANES)
    n1 = 0.9 * m1_ref[m] + 0.1 * flat
    n2 = 0.95 * m2_ref[m] + 0.05 * flat * flat
    n1_ref[...] = n1
    n2_ref[...] = n2
    up_ref[...] = (n1 / (jnp.sqrt(n2) + 1e-08)).astype(BF16)
    for k, (here, there) in enumerate(((n1_ref, n1_hbm), (n2_ref, n2_hbm), (up_ref, up_hbm), (q_ref, q_hbm))):
        copies.append(pltpu.make_async_copy(here, there.at[m], sem.at[k]))
        copies[-1].start()
    for copy in copies:
        copy.wait()


def update(pieces, hat, rows, full, moment1, moment2, mine, before=()):
    projections, depth, columns = full.shape
    slots, height, _ = pieces.shape
    state, tiles = moment1.shape[1], columns // LANES
    return pl.pallas_call(
        functools.partial(update_kernel, mine),
        in_specs=[WHOLE] * 6 + [AWAY] * len(before),
        out_specs=[AWAY] * 5,
        out_shape=[
            pltpu.HBM((1, projections, depth, columns), F32),
            pltpu.HBM(moment1.shape, F32),
            pltpu.HBM(moment2.shape, F32),
            pltpu.HBM(moment1.shape, BF16),
            pltpu.HBM((projections, RANK, columns), F32),
        ],
        scratch_shapes=[
            pltpu.VMEM((slots, depth, columns // slots), F32),
            pltpu.VMEM((state, LANES), F32),
            pltpu.VMEM((state, LANES), F32),
            pltpu.VMEM((state, LANES), BF16),
            pltpu.VMEM((RANK, columns), F32),
            pltpu.VMEM((tiles, 8, LANES), F32),
            pltpu.VMEM((state // tiles, tiles, LANES), F32),
            pltpu.SemaphoreType.DMA((slots,)),
            pltpu.SemaphoreType.DMA((4,)),
        ],
        input_output_aliases={6 + k: k for k in range(len(before))},
        compiler_params=PARAMS,
        cost_estimate=pl.CostEstimate(flops=100_000_000, bytes_accessed=4_000_000, transcendentals=30_000),
        name="update_own" if mine else "update_other",
    )(pieces, hat, rows, full, moment1, moment2, *before)


def swap(value, axis, bit):
    return lax.ppermute(value, axis, [(i, i ^ bit) for i in range(lax.axis_size(axis))])


def four(values, axis):
    return (values[0] + swap(values[1], axis, 1)) + (swap(values[2], axis, 2) + swap(values[3], axis, 3))


def shards(grads, errors, q_prev, moment1, moment2):
    replicas, slots = lax.axis_size(("z", "y")), lax.axis_size("x")
    full, p = left_factors(grads, errors, q_prev)
    p = four([p] * 4, "y")
    p = four([p] * 4, "z")
    p = p + swap(p, "z", 6)

    terms = swap(right_terms(p, full, replicas, slots, False), "c", 1) + right_terms(p, full, replicas, slots, True)
    total = four([terms[i] for i in range(slots)], "x")
    inverse = inverse_factor(total)
    q = four([total[:-8]] * 4, "y")
    q, inverse = lax.optimization_barrier((q, inverse))
    hat, rows = orthonormal(p, inverse, swap(inverse, "c", 1), replicas)
    q = four([q] * 4, "z")
    q, hat, rows = lax.optimization_barrier((q, hat, rows))
    piece = finished_piece(q, swap(q, "z", 6), inverse, replicas)
    own = jnp.stack([piece] + [swap(piece, "x", i) for i in range(1, slots)])
    other = swap(own, "c", 1)
    done = update(own, hat, rows, full, moment1, moment2, True)
    return tuple(update(other, hat, rows, full, moment1, moment2, False, done))


def solution(mesh):
    mesh = Mesh(mesh.devices.reshape(8, 4, 4, 2), ("z", "y", "x", "c"))
    dp, fsdp = ("z", "y"), ("x", "c")
    blocks = P(dp, None, fsdp, None)
    states = P(None, fsdp + dp, None)
    return jax.shard_map(
        shards,
        mesh=mesh,
        in_specs=(blocks, blocks, P(), states, states),
        out_specs=(blocks, states, states, states, P()),
        check_vma=False,
    )
```

```python
import functools

import jax
import jax.numpy as jnp
from jax import lax
from jax.experimental import pallas as pl
from jax.experimental.pallas import tpu as pltpu
from jax.sharding import Mesh, PartitionSpec as P

F32 = jnp.float32
BF16 = jnp.bfloat16
RANK = 32
LANES = 128
VMEM_LIMIT = 24 * 2**20
PARAMS = pltpu.CompilerParams(vmem_limit_bytes=VMEM_LIMIT)
WHOLE = pl.BlockSpec(memory_space=pltpu.VMEM)
AWAY = pl.BlockSpec(memory_space=pl.ANY)


def in_hbm(x):
    return pltpu.with_memory_space_constraint(x, pltpu.HBM)


def split(x):
    head = x.astype(BF16)
    return head, (x - head.astype(F32)).astype(BF16)


def left_three(x):
    hi, lo = split(x)
    return jnp.concatenate([hi, lo, hi], axis=1)


def right_three(x):
    hi, lo = split(x)
    return jnp.concatenate([hi, hi, lo], axis=0)


def dot(a, b, a_dim, b_dim, precision=None):
    return lax.dot_general(a, b, (((a_dim,), (b_dim,)), ((), ())), precision=precision, preferred_element_type=F32)


def pack(square):
    return jnp.concatenate([square[8 * i : 8 * i + 8] for i in range(4)], axis=1)


def unpack(packed):
    return jnp.concatenate([packed[:, 32 * i : 32 * i + 32] for i in range(4)], axis=0)


def pack_rows(columns):
    rows = columns.shape[0] // 4
    return jnp.concatenate([columns[rows * i : rows * (i + 1)] for i in range(4)], axis=1)


def unpack_rows(packed):
    return jnp.concatenate([packed[:, RANK * i : RANK * (i + 1)] for i in range(4)], axis=0)


def left_kernel(grads_hbm, errors_hbm, q_hbm, other_ref, own_ref, p_other_ref, p_own_ref, grads_ref, q_ref, grads_sem, errors_sem, q_sem):
    core = lax.axis_index("c")
    parts = ((1 - core, other_ref, p_other_ref), (core, own_ref, p_own_ref))
    q_copy = pltpu.make_async_copy(q_hbm, q_ref, q_sem)
    copies = [
        (
            pltpu.make_async_copy(grads_hbm.at[0, m], grads_ref.at[i], grads_sem.at[i]),
            pltpu.make_async_copy(errors_hbm.at[0, m], full_ref, errors_sem.at[i]),
        )
        for i, (m, full_ref, _) in enumerate(parts)
    ]
    q_copy.start()
    for pair in copies:
        for copy in pair:
            copy.start()
    q_copy.wait()
    for i, (m, full_ref, p_ref) in enumerate(parts):
        q_hi, q_lo = split(q_ref[m])
        both = jnp.concatenate([q_hi, q_lo], axis=0)
        for copy in copies[i]:
            copy.wait()
        full = grads_ref[i].astype(F32) + full_ref[...]
        full_ref[...] = full
        f_hi, f_lo = split(full)
        wide = dot(f_hi, both, 1, 1)
        p_ref[...] = pack_rows(wide[:, :RANK] + wide[:, RANK:] + dot(f_lo, q_hi, 1, 1))


def left_factors(grads, errors, q_prev):
    _, projections, rows, columns = grads.shape
    full, p = pltpu.VMEM((rows, columns), F32), pltpu.VMEM((rows // 4, LANES), F32)
    return pl.pallas_call(
        left_kernel,
        in_specs=[AWAY] * 3,
        out_specs=[WHOLE] * 4,
        out_shape=[full, full, p, p],
        scratch_shapes=[
            pltpu.VMEM((projections, rows, columns), BF16),
            pltpu.VMEM(q_prev.shape, F32),
            pltpu.SemaphoreType.DMA((projections,)),
            pltpu.SemaphoreType.DMA((projections,)),
            pltpu.SemaphoreType.DMA,
        ],
        compiler_params=PARAMS,
        name="left_factors",
    )(in_hbm(grads), in_hbm(errors), in_hbm(q_prev))


def right_kernel(replicas, p_ref, own_ref, gift_ref, out_ref):
    slots, height, _ = out_ref.shape
    tiles = (height - 8) // RANK
    width = tiles * LANES
    x = lax.axis_index("x")
    half = p_ref.shape[0] // 2
    columns = jnp.concatenate([unpack_rows(p_ref[:half]), unpack_rows(p_ref[half:])], axis=0)
    p = (columns * (1.0 / replicas)).T
    p_hi, p_lo = split(p)
    both = jnp.concatenate([p_hi, p_lo], axis=0)
    gram = pack(dot(p, p, 1, 1, lax.Precision.HIGHEST))
    for slot in range(slots):
        here = pl.ds(pl.multiple_of((x ^ slot) * width, width), width)
        f_hi, f_lo = split(jnp.concatenate([own_ref[:, here], gift_ref[:, here]], axis=0))
        wide = dot(both, f_hi, 1, 0)
        q = wide[:RANK] + wide[RANK:] + dot(p_hi, f_lo, 1, 0)
        for j in range(tiles):
            out_ref[slot, j * RANK : (j + 1) * RANK, :] = q[:, j * LANES : (j + 1) * LANES]
        out_ref[slot, tiles * RANK :, :] = gram


def right_terms(p_sum, own, gift, replicas, slots):
    height = own.shape[1] // slots // LANES * RANK + 8
    return pl.pallas_call(
        functools.partial(right_kernel, replicas),
        in_specs=[WHOLE] * 3,
        out_specs=WHOLE,
        out_shape=jax.ShapeDtypeStruct((slots, height, LANES), F32),
        compiler_params=PARAMS,
        name="right_terms",
    )(p_sum, own, gift)


def factor_kernel(sum_ref, out_ref):
    gram = unpack(sum_ref[sum_ref.shape[0] - 8 :, :])
    row = lax.broadcasted_iota(jnp.int32, (RANK, RANK), 0)
    column = lax.broadcasted_iota(jnp.int32, (RANK, RANK), 1)
    work = jnp.concatenate([gram, (row == column).astype(F32)], axis=1)
    below = lax.broadcasted_iota(jnp.int32, (RANK, 2 * RANK), 0)
    scale = jnp.zeros((RANK, 1), F32)
    first = lax.broadcasted_iota(jnp.int32, (RANK, 1), 0)
    for k in range(RANK):
        top = work[k : k + 1, :]
        pivot = work[k : k + 1, k : k + 1]
        scale = jnp.where(first == k, lax.rsqrt(pivot), scale)
        if k < RANK - 1:
            ratio = work[:, k : k + 1] * (1.0 / pivot)
            work = jnp.where(below > k, work - ratio * top, work)
    out_ref[...] = pack(work[:, RANK:] * scale)


def inverse_factor(total):
    return pl.pallas_call(
        factor_kernel,
        in_specs=[WHOLE],
        out_specs=WHOLE,
        out_shape=jax.ShapeDtypeStruct((8, LANES), F32),
        compiler_params=PARAMS,
        cost_estimate=pl.CostEstimate(flops=4_000_000, bytes_accessed=4_000_000, transcendentals=64),
        name="inverse_factor",
    )(total)


def hat_kernel(replicas, p_ref, inverse_ref, own_ref, other_ref):
    half = p_ref.shape[0] // 2
    inverse = unpack(inverse_ref[...])
    for i, out_ref in enumerate((own_ref, other_ref)):
        p = unpack_rows(p_ref[half * i : half * (i + 1)]) * (1.0 / replicas)
        out_ref[...] = pack_rows(dot(p, inverse, 1, 1, lax.Precision.HIGHEST))


def orthonormal(p_sum, inverse, replicas):
    half = jax.ShapeDtypeStruct((p_sum.shape[0] // 2, LANES), F32)
    return pl.pallas_call(
        functools.partial(hat_kernel, replicas),
        in_specs=[WHOLE] * 2,
        out_specs=[WHOLE] * 2,
        out_shape=[half, half],
        compiler_params=PARAMS,
        cost_estimate=pl.CostEstimate(flops=4_000_000, bytes_accessed=1_000_000, transcendentals=64),
        name="orthonormal",
    )(p_sum, inverse)


def side_kernel(replicas, own_ref, other_ref, hat_ref, rows_ref):
    rows = hat_ref.shape[1]
    at = lax.broadcasted_iota(jnp.int32, (16, rows), 0) + lax.axis_index(("z", "y")) * (rows // replicas)
    chosen = (lax.broadcasted_iota(jnp.int32, (16, rows), 1) == at).astype(F32)
    for i, ref in enumerate((own_ref, other_ref)):
        hat = unpack_rows(ref[...])
        hat_ref[i] = left_three(hat)
        rows_ref[i] = left_three(dot(chosen, hat, 1, 0, lax.Precision.HIGHEST))


def left_sides(own, other, replicas):
    rows = 4 * own.shape[0]
    return pl.pallas_call(
        functools.partial(side_kernel, replicas),
        in_specs=[WHOLE] * 2,
        out_specs=[WHOLE] * 2,
        out_shape=[jax.ShapeDtypeStruct((2, rows, 3 * RANK), BF16), jax.ShapeDtypeStruct((2, 16, 3 * RANK), BF16)],
        compiler_params=PARAMS,
        cost_estimate=pl.CostEstimate(flops=4_000_000, bytes_accessed=1_000_000, transcendentals=64),
        name="left_sides",
    )(own, other)


def piece_kernel(replicas, a_ref, b_ref, inverse_ref, out_ref):
    inverse = unpack(inverse_ref[...]) * (1.0 / replicas)
    tiles = a_ref.shape[0] // RANK
    rows = a_ref[...] + b_ref[...]
    wide = jnp.concatenate([rows[j * RANK : (j + 1) * RANK] for j in range(tiles)], axis=1)
    q = dot(inverse, wide, 1, 0, lax.Precision.HIGHEST)
    for j in range(tiles):
        out_ref[j * RANK : (j + 1) * RANK, :] = q[:, j * LANES : (j + 1) * LANES]


def finished_piece(a, b, inverse, replicas):
    return pl.pallas_call(
        functools.partial(piece_kernel, replicas),
        in_specs=[WHOLE] * 3,
        out_specs=WHOLE,
        out_shape=jax.ShapeDtypeStruct(a.shape, F32),
        compiler_params=PARAMS,
        name="finished_piece",
    )(a, b, inverse)


def update_kernel(mine, pieces_ref, hat_ref, rows_ref, full_ref, m1_ref, m2_ref, *refs):
    err_hbm, n1_hbm, n2_hbm, up_hbm, q_hbm, err_ref, n1_ref, n2_ref, up_ref, q_ref, tile_ref, flat_ref, err_sem, sem = refs[-14:]
    slots, height, _ = pieces_ref.shape
    tiles = height // RANK
    width = tiles * LANES
    x, core = lax.axis_index("x"), lax.axis_index("c")
    i, m = (0, core) if mine else (1, 1 - core)
    copies = []
    for slot in range(slots):
        block = x ^ slot
        here = pl.ds(pl.multiple_of(block * width, width), width)
        q = jnp.concatenate([pieces_ref[slot, j * RANK : (j + 1) * RANK, :] for j in range(tiles)], axis=1)
        right = right_three(q)
        err_ref[slot] = full_ref[:, here] - dot(hat_ref[i], right, 1, 0)
        copies.append(pltpu.make_async_copy(err_ref.at[slot], err_hbm.at[0, m, :, here], err_sem.at[slot]))
        copies[-1].start()
        q_ref[:, here] = q
        state = dot(rows_ref[i], right, 1, 0)
        for j in range(tiles):
            tile_ref[block * tiles + j] = state[:8, j * LANES : (j + 1) * LANES]
    share = flat_ref.shape[0]
    for j in range(slots * tiles):
        flat_ref[:, j, :] = tile_ref[j, :share, :]
    flat = flat_ref[...].reshape(share * slots * tiles, LANES)
    n1 = 0.9 * m1_ref[m] + 0.1 * flat
    n2 = 0.95 * m2_ref[m] + 0.05 * flat * flat
    n1_ref[...] = n1
    n2_ref[...] = n2
    up_ref[...] = (n1 / (jnp.sqrt(n2) + 1e-08)).astype(BF16)
    for k, (here, there) in enumerate(((n1_ref, n1_hbm), (n2_ref, n2_hbm), (up_ref, up_hbm), (q_ref, q_hbm))):
        copies.append(pltpu.make_async_copy(here, there.at[m], sem.at[k]))
        copies[-1].start()
    for copy in copies:
        copy.wait()


def update(pieces, hat, rows, full, moment1, moment2, mine, before=()):
    depth, columns = full.shape
    projections, slots = hat.shape[0], pieces.shape[0]
    state, tiles = moment1.shape[1], columns // LANES
    return pl.pallas_call(
        functools.partial(update_kernel, mine),
        in_specs=[WHOLE] * 6 + [AWAY] * len(before),
        out_specs=[AWAY] * 5,
        out_shape=[
            pltpu.HBM((1, projections, depth, columns), F32),
            pltpu.HBM(moment1.shape, F32),
            pltpu.HBM(moment2.shape, F32),
            pltpu.HBM(moment1.shape, BF16),
            pltpu.HBM((projections, RANK, columns), F32),
        ],
        scratch_shapes=[
            pltpu.VMEM((slots, depth, columns // slots), F32),
            pltpu.VMEM((state, LANES), F32),
            pltpu.VMEM((state, LANES), F32),
            pltpu.VMEM((state, LANES), BF16),
            pltpu.VMEM((RANK, columns), F32),
            pltpu.VMEM((tiles, 8, LANES), F32),
            pltpu.VMEM((state // tiles, tiles, LANES), F32),
            pltpu.SemaphoreType.DMA((slots,)),
            pltpu.SemaphoreType.DMA((4,)),
        ],
        input_output_aliases={6 + k: k for k in range(len(before))},
        compiler_params=PARAMS,
        cost_estimate=pl.CostEstimate(flops=100_000_000, bytes_accessed=4_000_000, transcendentals=30_000),
        name="update_own" if mine else "update_other",
    )(pieces, hat, rows, full, moment1, moment2, *before)


def swap(value, axis, bit):
    return lax.ppermute(value, axis, [(i, i ^ bit) for i in range(lax.axis_size(axis))])


def four(values, axis):
    return (values[0] + swap(values[1], axis, 1)) + (swap(values[2], axis, 2) + swap(values[3], axis, 3))


def shards(grads, errors, q_prev, moment1, moment2):
    replicas, slots = lax.axis_size(("z", "y")), lax.axis_size("x")
    other_full, own_full, p_other, p_own = left_factors(grads, errors, q_prev)
    p = jnp.concatenate([p_own, swap(p_other, "c", 1)])
    p, other_full = lax.optimization_barrier((p, other_full))
    gift = swap(other_full, "c", 1)
    p = four([p] * 4, "y")
    p = four([p] * 4, "z")
    p = p + swap(p, "z", 6)

    terms = right_terms(p, own_full, gift, replicas, slots)
    total = four([terms[i] for i in range(slots)], "x")
    inverse = inverse_factor(total)
    q = four([total[:-8]] * 4, "y")
    q, inverse = lax.optimization_barrier((q, inverse))
    hat_own, hat_other = orthonormal(p, inverse, replicas)
    hat_gift = swap(hat_other, "c", 1)
    q = four([q] * 4, "z")
    q, hat_own, hat_gift = lax.optimization_barrier((q, hat_own, hat_gift))
    hat, rows = left_sides(hat_own, hat_gift, replicas)
    far, hat, rows = lax.optimization_barrier((swap(q, "z", 6), hat, rows))
    piece = finished_piece(q, far, inverse, replicas)
    own = jnp.stack([piece] + [swap(piece, "x", i) for i in range(1, slots)])
    other = swap(own, "c", 1)
    done = update(own, hat, rows, own_full, moment1, moment2, True)
    return tuple(update(other, hat, rows, other_full, moment1, moment2, False, done))


def solution(mesh):
    mesh = Mesh(mesh.devices.reshape(8, 4, 4, 2), ("z", "y", "x", "c"))
    dp, fsdp = ("z", "y"), ("x", "c")
    blocks = P(dp, None, fsdp, None)
    states = P(None, fsdp + dp, None)
    return jax.shard_map(
        shards,
        mesh=mesh,
        in_specs=(blocks, blocks, P(), states, states),
        out_specs=(blocks, states, states, states, P()),
        check_vma=False,
    )
```

```python
import functools

import jax
import jax.numpy as jnp
import numpy as np
from jax import lax
from jax.experimental import pallas as pl
from jax.experimental.pallas import tpu as pltpu
from jax.sharding import Mesh, PartitionSpec as P

F32 = jnp.float32
BF16 = jnp.bfloat16
RANK = 32
LANES = 128
VMEM_LIMIT = 24 * 2**20
PARAMS = pltpu.CompilerParams(vmem_limit_bytes=VMEM_LIMIT)
WHOLE = pl.BlockSpec(memory_space=pltpu.VMEM)
AWAY = pl.BlockSpec(memory_space=pl.ANY)


def in_hbm(x):
    return pltpu.with_memory_space_constraint(x, pltpu.HBM)


def split(x):
    head = x.astype(BF16)
    return head, (x - head.astype(F32)).astype(BF16)


def left_three(x):
    hi, lo = split(x)
    return jnp.concatenate([hi, lo, hi], axis=1)


def right_three(x):
    hi, lo = split(x)
    return jnp.concatenate([hi, hi, lo], axis=0)


def dot(a, b, a_dim, b_dim, precision=None):
    return lax.dot_general(a, b, (((a_dim,), (b_dim,)), ((), ())), precision=precision, preferred_element_type=F32)


def pack(square):
    return jnp.concatenate([square[8 * i : 8 * i + 8] for i in range(4)], axis=1)


def unpack(packed):
    return jnp.concatenate([packed[:, 32 * i : 32 * i + 32] for i in range(4)], axis=0)


def pack_rows(columns):
    rows = columns.shape[0] // 4
    return jnp.concatenate([columns[rows * i : rows * (i + 1)] for i in range(4)], axis=1)


def unpack_rows(packed):
    return jnp.concatenate([packed[:, RANK * i : RANK * (i + 1)] for i in range(4)], axis=0)


def left_kernel(grads_hbm, errors_hbm, q_hbm, other_ref, own_ref, p_other_ref, p_own_ref, grads_ref, q_ref, grads_sem, errors_sem, q_sem):
    core = lax.axis_index("c")
    parts = ((1 - core, other_ref, p_other_ref), (core, own_ref, p_own_ref))
    q_copy = pltpu.make_async_copy(q_hbm, q_ref, q_sem)
    copies = [
        (
            pltpu.make_async_copy(grads_hbm.at[0, m], grads_ref.at[i], grads_sem.at[i]),
            pltpu.make_async_copy(errors_hbm.at[0, m], full_ref, errors_sem.at[i]),
        )
        for i, (m, full_ref, _) in enumerate(parts)
    ]
    q_copy.start()
    for pair in copies:
        for copy in pair:
            copy.start()
    q_copy.wait()
    for i, (m, full_ref, p_ref) in enumerate(parts):
        q_hi, q_lo = split(q_ref[m])
        both = jnp.concatenate([q_hi, q_lo], axis=0)
        for copy in copies[i]:
            copy.wait()
        full = grads_ref[i].astype(F32) + full_ref[...]
        full_ref[...] = full
        f_hi, f_lo = split(full)
        wide = dot(f_hi, both, 1, 1)
        p_ref[...] = pack_rows(wide[:, :RANK] + wide[:, RANK:] + dot(f_lo, q_hi, 1, 1))


def left_factors(grads, errors, q_prev):
    _, projections, rows, columns = grads.shape
    full, p = pltpu.VMEM((rows, columns), F32), pltpu.VMEM((rows // 4, LANES), F32)
    return pl.pallas_call(
        left_kernel,
        in_specs=[AWAY] * 3,
        out_specs=[WHOLE] * 4,
        out_shape=[full, full, p, p],
        scratch_shapes=[
            pltpu.VMEM((projections, rows, columns), BF16),
            pltpu.VMEM(q_prev.shape, F32),
            pltpu.SemaphoreType.DMA((projections,)),
            pltpu.SemaphoreType.DMA((projections,)),
            pltpu.SemaphoreType.DMA,
        ],
        compiler_params=PARAMS,
        name="left_factors",
    )(in_hbm(grads), in_hbm(errors), in_hbm(q_prev))


def block_place(core):
    return jnp.where(core == 0, lax.axis_index("x"), lax.axis_index("y"))


def right_kernel(replicas, p_ref, own_ref, gift_ref, out_ref):
    slots, height, _ = out_ref.shape
    tiles = (height - 8) // RANK
    width = tiles * LANES
    place = block_place(lax.axis_index("c"))
    half = p_ref.shape[0] // 2
    columns = jnp.concatenate([unpack_rows(p_ref[:half]), unpack_rows(p_ref[half:])], axis=0)
    p = (columns * (1.0 / replicas)).T
    p_hi, p_lo = split(p)
    both = jnp.concatenate([p_hi, p_lo], axis=0)
    gram = pack(dot(p, p, 1, 1, lax.Precision.HIGHEST))
    for slot in range(slots):
        here = pl.ds(pl.multiple_of((place ^ slot) * width, width), width)
        f_hi, f_lo = split(jnp.concatenate([own_ref[:, here], gift_ref[:, here]], axis=0))
        wide = dot(both, f_hi, 1, 0)
        q = wide[:RANK] + wide[RANK:] + dot(p_hi, f_lo, 1, 0)
        for j in range(tiles):
            out_ref[slot, j * RANK : (j + 1) * RANK, :] = q[:, j * LANES : (j + 1) * LANES]
        out_ref[slot, tiles * RANK :, :] = gram


def right_terms(p_sum, own, gift, replicas, slots):
    height = own.shape[1] // slots // LANES * RANK + 8
    return pl.pallas_call(
        functools.partial(right_kernel, replicas),
        in_specs=[WHOLE] * 3,
        out_specs=WHOLE,
        out_shape=jax.ShapeDtypeStruct((slots, height, LANES), F32),
        compiler_params=PARAMS,
        name="right_terms",
    )(p_sum, own, gift)


def factor_kernel(copies, sum_ref, out_ref):
    gram = unpack(sum_ref[sum_ref.shape[0] - 8 :, :]) * (1.0 / copies)
    row = lax.broadcasted_iota(jnp.int32, (RANK, RANK), 0)
    column = lax.broadcasted_iota(jnp.int32, (RANK, RANK), 1)
    work = jnp.concatenate([gram, (row == column).astype(F32)], axis=1)
    below = lax.broadcasted_iota(jnp.int32, (RANK, 2 * RANK), 0)
    scale = jnp.zeros((RANK, 1), F32)
    first = lax.broadcasted_iota(jnp.int32, (RANK, 1), 0)
    for k in range(RANK):
        top = work[k : k + 1, :]
        pivot = work[k : k + 1, k : k + 1]
        scale = jnp.where(first == k, lax.rsqrt(pivot), scale)
        if k < RANK - 1:
            ratio = work[:, k : k + 1] * (1.0 / pivot)
            work = jnp.where(below > k, work - ratio * top, work)
    out_ref[...] = pack(work[:, RANK:] * scale)


def inverse_factor(total, copies):
    return pl.pallas_call(
        functools.partial(factor_kernel, copies),
        in_specs=[WHOLE],
        out_specs=WHOLE,
        out_shape=jax.ShapeDtypeStruct((8, LANES), F32),
        compiler_params=PARAMS,
        cost_estimate=pl.CostEstimate(flops=4_000_000, bytes_accessed=4_000_000, transcendentals=64),
        name="inverse_factor",
    )(total)


def hat_kernel(replicas, p_ref, inverse_ref, own_ref, other_ref):
    half = p_ref.shape[0] // 2
    inverse = unpack(inverse_ref[...])
    for i, out_ref in enumerate((own_ref, other_ref)):
        p = unpack_rows(p_ref[half * i : half * (i + 1)]) * (1.0 / replicas)
        out_ref[...] = pack_rows(dot(p, inverse, 1, 1, lax.Precision.HIGHEST))


def orthonormal(p_sum, inverse, replicas):
    half = jax.ShapeDtypeStruct((p_sum.shape[0] // 2, LANES), F32)
    return pl.pallas_call(
        functools.partial(hat_kernel, replicas),
        in_specs=[WHOLE] * 2,
        out_specs=[WHOLE] * 2,
        out_shape=[half, half],
        compiler_params=PARAMS,
        cost_estimate=pl.CostEstimate(flops=4_000_000, bytes_accessed=1_000_000, transcendentals=64),
        name="orthonormal",
    )(p_sum, inverse)


def side_kernel(replicas, own_ref, other_ref, hat_ref, rows_ref):
    rows = hat_ref.shape[1]
    at = lax.broadcasted_iota(jnp.int32, (16, rows), 0) + lax.axis_index(("z", "y")) * (rows // replicas)
    chosen = (lax.broadcasted_iota(jnp.int32, (16, rows), 1) == at).astype(F32)
    for i, ref in enumerate((own_ref, other_ref)):
        hat = unpack_rows(ref[...])
        hat_ref[i] = left_three(hat)
        rows_ref[i] = left_three(dot(chosen, hat, 1, 0, lax.Precision.HIGHEST))


def left_sides(own, other, replicas):
    rows = 4 * own.shape[0]
    return pl.pallas_call(
        functools.partial(side_kernel, replicas),
        in_specs=[WHOLE] * 2,
        out_specs=[WHOLE] * 2,
        out_shape=[jax.ShapeDtypeStruct((2, rows, 3 * RANK), BF16), jax.ShapeDtypeStruct((2, 16, 3 * RANK), BF16)],
        compiler_params=PARAMS,
        cost_estimate=pl.CostEstimate(flops=4_000_000, bytes_accessed=1_000_000, transcendentals=64),
        name="left_sides",
    )(own, other)


def piece_kernel(replicas, a_ref, b_ref, inverse_ref, out_ref):
    inverse = unpack(inverse_ref[...]) * (1.0 / replicas)
    tiles = a_ref.shape[0] // RANK
    rows = a_ref[...] + b_ref[...]
    wide = jnp.concatenate([rows[j * RANK : (j + 1) * RANK] for j in range(tiles)], axis=1)
    q = dot(inverse, wide, 1, 0, lax.Precision.HIGHEST)
    for j in range(tiles):
        out_ref[j * RANK : (j + 1) * RANK, :] = q[:, j * LANES : (j + 1) * LANES]


def finished_piece(a, b, inverse, replicas):
    return pl.pallas_call(
        functools.partial(piece_kernel, replicas),
        in_specs=[WHOLE] * 3,
        out_specs=WHOLE,
        out_shape=jax.ShapeDtypeStruct(a.shape, F32),
        compiler_params=PARAMS,
        name="finished_piece",
    )(a, b, inverse)


def update_kernel(mine, pieces_ref, hat_ref, rows_ref, full_ref, m1_ref, m2_ref, *refs):
    err_hbm, n1_hbm, n2_hbm, up_hbm, q_hbm, err_ref, n1_ref, n2_ref, up_ref, q_ref, tile_ref, flat_ref, err_sem, sem = refs[-14:]
    slots, height, _ = pieces_ref.shape
    tiles = height // RANK
    width = tiles * LANES
    core = lax.axis_index("c")
    i, m = (0, core) if mine else (1, 1 - core)
    place = block_place(m)
    copies = []
    for slot in range(slots):
        block = place ^ slot
        here = pl.ds(pl.multiple_of(block * width, width), width)
        q = jnp.concatenate([pieces_ref[slot, j * RANK : (j + 1) * RANK, :] for j in range(tiles)], axis=1)
        right = right_three(q)
        err_ref[slot] = full_ref[:, here] - dot(hat_ref[i], right, 1, 0)
        copies.append(pltpu.make_async_copy(err_ref.at[slot], err_hbm.at[0, m, :, here], err_sem.at[slot]))
        copies[-1].start()
        q_ref[:, here] = q
        state = dot(rows_ref[i], right, 1, 0)
        for j in range(tiles):
            tile_ref[block * tiles + j] = state[:8, j * LANES : (j + 1) * LANES]
    share = flat_ref.shape[0]
    for j in range(slots * tiles):
        flat_ref[:, j, :] = tile_ref[j, :share, :]
    flat = flat_ref[...].reshape(share * slots * tiles, LANES)
    n1 = 0.9 * m1_ref[m] + 0.1 * flat
    n2 = 0.95 * m2_ref[m] + 0.05 * flat * flat
    n1_ref[...] = n1
    n2_ref[...] = n2
    up_ref[...] = (n1 / (jnp.sqrt(n2) + 1e-08)).astype(BF16)
    for k, (here, there) in enumerate(((n1_ref, n1_hbm), (n2_ref, n2_hbm), (up_ref, up_hbm), (q_ref, q_hbm))):
        copies.append(pltpu.make_async_copy(here, there.at[m], sem.at[k]))
        copies[-1].start()
    for copy in copies:
        copy.wait()


def update(pieces, hat, rows, full, moment1, moment2, mine, before=()):
    depth, columns = full.shape
    projections, slots = hat.shape[0], pieces.shape[0]
    state, tiles = moment1.shape[1], columns // LANES
    return pl.pallas_call(
        functools.partial(update_kernel, mine),
        in_specs=[WHOLE] * 6 + [AWAY] * len(before),
        out_specs=[AWAY] * 5,
        out_shape=[
            pltpu.HBM((1, projections, depth, columns), F32),
            pltpu.HBM(moment1.shape, F32),
            pltpu.HBM(moment2.shape, F32),
            pltpu.HBM(moment1.shape, BF16),
            pltpu.HBM((projections, RANK, columns), F32),
        ],
        scratch_shapes=[
            pltpu.VMEM((slots, depth, columns // slots), F32),
            pltpu.VMEM((state, LANES), F32),
            pltpu.VMEM((state, LANES), F32),
            pltpu.VMEM((state, LANES), BF16),
            pltpu.VMEM((RANK, columns), F32),
            pltpu.VMEM((tiles, 8, LANES), F32),
            pltpu.VMEM((state // tiles, tiles, LANES), F32),
            pltpu.SemaphoreType.DMA((slots,)),
            pltpu.SemaphoreType.DMA((4,)),
        ],
        input_output_aliases={6 + k: k for k in range(len(before))},
        compiler_params=PARAMS,
        cost_estimate=pl.CostEstimate(flops=100_000_000, bytes_accessed=4_000_000, transcendentals=30_000),
        name="update_own" if mine else "update_other",
    )(pieces, hat, rows, full, moment1, moment2, *before)


def swap(value, axes, bit):
    names = ("z", "y", "x", "c")
    sizes = tuple(lax.axis_size(name) for name in names)
    pairs = []
    for here in np.ndindex(*sizes):
        there = list(here)
        there[names.index(axes[here[-1]])] ^= bit
        pairs.append((int(np.ravel_multi_index(here, sizes)), int(np.ravel_multi_index(there, sizes))))
    return lax.ppermute(value, names, pairs)


def four(values, axes):
    return (values[0] + swap(values[1], axes, 1)) + (swap(values[2], axes, 2) + swap(values[3], axes, 3))


def shards(grads, errors, q_prev, moment1, moment2):
    replicas, slots = lax.axis_size(("z", "y")), lax.axis_size("x")
    other_full, own_full, p_other, p_own = left_factors(grads, errors, q_prev)
    p = jnp.concatenate([p_own, swap(p_other, "cc", 1)])
    p, other_full = lax.optimization_barrier((p, other_full))
    gift = swap(other_full, "cc", 1)
    p = four([p] * 4, "yz")
    p = four([p] * 4, "zy")
    p = p + swap(p, "zz", 6)

    terms = right_terms(p, own_full, gift, replicas, slots)
    total = four([terms[i] for i in range(slots)], "xy")
    total = four([total] * 4, "zx")
    inverse = inverse_factor(total, slots)
    q = four([total[:-8]] * 4, "yz")
    q, inverse = lax.optimization_barrier((q, inverse))
    hat_own, hat_other = orthonormal(p, inverse, replicas)
    hat, rows = left_sides(hat_own, swap(hat_other, "cc", 1), replicas)
    far, hat, rows = lax.optimization_barrier((swap(q, "zz", 6), hat, rows))
    piece = finished_piece(q, far, inverse, replicas)
    own = jnp.stack([piece] + [swap(piece, "xy", i) for i in range(1, slots)])
    other = swap(own, "cc", 1)
    done = update(own, hat, rows, own_full, moment1, moment2, True)
    return tuple(update(other, hat, rows, other_full, moment1, moment2, False, done))


def solution(mesh):
    mesh = Mesh(mesh.devices.reshape(8, 4, 4, 2), ("z", "y", "x", "c"))
    dp, fsdp = ("z", "y"), ("x", "c")
    blocks = P(dp, None, fsdp, None)
    states = P(None, fsdp + dp, None)
    return jax.shard_map(
        shards,
        mesh=mesh,
        in_specs=(blocks, blocks, P(), states, states),
        out_specs=(blocks, states, states, states, P()),
        check_vma=False,
    )
```

```python
import functools

import jax
import jax.numpy as jnp
import numpy as np
from jax import lax
from jax.experimental import pallas as pl
from jax.experimental.pallas import tpu as pltpu
from jax.sharding import Mesh, PartitionSpec as P

F32 = jnp.float32
BF16 = jnp.bfloat16
RANK = 32
LANES = 128
VMEM_LIMIT = 24 * 2**20
PARAMS = pltpu.CompilerParams(vmem_limit_bytes=VMEM_LIMIT)
WHOLE = pl.BlockSpec(memory_space=pltpu.VMEM)
AWAY = pl.BlockSpec(memory_space=pl.ANY)


def in_hbm(x):
    return pltpu.with_memory_space_constraint(x, pltpu.HBM)


def split(x):
    head = x.astype(BF16)
    return head, (x - head.astype(F32)).astype(BF16)


def left_three(x):
    hi, lo = split(x)
    return jnp.concatenate([hi, lo, hi], axis=1)


def right_three(x):
    hi, lo = split(x)
    return jnp.concatenate([hi, hi, lo], axis=0)


def dot(a, b, a_dim, b_dim, precision=None):
    return lax.dot_general(a, b, (((a_dim,), (b_dim,)), ((), ())), precision=precision, preferred_element_type=F32)


def pack(square):
    return jnp.concatenate([square[8 * i : 8 * i + 8] for i in range(4)], axis=1)


def unpack(packed):
    return jnp.concatenate([packed[:, 32 * i : 32 * i + 32] for i in range(4)], axis=0)


def pack_rows(columns):
    rows = columns.shape[0] // 4
    return jnp.concatenate([columns[rows * i : rows * (i + 1)] for i in range(4)], axis=1)


def unpack_rows(packed):
    return jnp.concatenate([packed[:, RANK * i : RANK * (i + 1)] for i in range(4)], axis=0)


def lane():
    return (lax.axis_index("c") + sum(lax.axis_index(name) // 2 for name in ("x", "y", "z"))) % 2


def left_kernel(grads_hbm, errors_hbm, q_hbm, other_ref, own_ref, p_send_ref, p_keep_ref, grads_ref, q_ref, grads_sem, errors_sem, q_sem):
    core, mine = lax.axis_index("c"), lane()
    parts = ((1 - mine, other_ref, p_send_ref), (mine, own_ref, p_keep_ref))
    q_copy = pltpu.make_async_copy(q_hbm, q_ref, q_sem)
    copies = [
        (
            pltpu.make_async_copy(grads_hbm.at[0, m], grads_ref.at[i], grads_sem.at[i]),
            pltpu.make_async_copy(errors_hbm.at[0, m], full_ref, errors_sem.at[i]),
        )
        for i, (m, full_ref, _) in enumerate(parts)
    ]
    q_copy.start()
    for pair in copies:
        for copy in pair:
            copy.start()
    q_copy.wait()
    for i, (m, full_ref, p_ref) in enumerate(parts):
        q_hi, q_lo = split(q_ref[m])
        both = jnp.concatenate([q_hi, q_lo], axis=0)
        for copy in copies[i]:
            copy.wait()
        full = grads_ref[i].astype(F32) + full_ref[...]
        full_ref[...] = full
        f_hi, f_lo = split(full)
        wide = dot(f_hi, both, 1, 1)
        p_ref[core] = pack_rows(wide[:, :RANK] + wide[:, RANK:] + dot(f_lo, q_hi, 1, 1))
        p_ref[1 - core] = jnp.zeros(p_ref.shape[1:], F32)


def left_factors(grads, errors, q_prev):
    _, projections, rows, columns = grads.shape
    full, p = pltpu.VMEM((rows, columns), F32), pltpu.VMEM((2, rows // 4, LANES), F32)
    return pl.pallas_call(
        left_kernel,
        in_specs=[AWAY] * 3,
        out_specs=[WHOLE] * 4,
        out_shape=[full, full, p, p],
        scratch_shapes=[
            pltpu.VMEM((projections, rows, columns), BF16),
            pltpu.VMEM(q_prev.shape, F32),
            pltpu.SemaphoreType.DMA((projections,)),
            pltpu.SemaphoreType.DMA((projections,)),
            pltpu.SemaphoreType.DMA,
        ],
        compiler_params=PARAMS,
        name="left_factors",
    )(in_hbm(grads), in_hbm(errors), in_hbm(q_prev))


def right_kernel(replicas, p_ref, own_ref, gift_ref, out_ref):
    slots, height, _ = out_ref.shape
    tiles = (height - 8) // RANK
    width = tiles * LANES
    x, core = lax.axis_index("x"), lax.axis_index("c")

    def factors(first, second):
        columns = jnp.concatenate([unpack_rows(p_ref[first]), unpack_rows(p_ref[second])], axis=0)
        return (columns * (1.0 / replicas)).T

    p = factors(0, 1)
    gram = pack(dot(p, p, 1, 1, lax.Precision.HIGHEST))
    p_hi, p_lo = split(factors(core, 1 - core))
    both = jnp.concatenate([p_hi, p_lo], axis=0)
    for slot in range(slots):
        here = pl.ds(pl.multiple_of((x ^ slot) * width, width), width)
        f_hi, f_lo = split(jnp.concatenate([own_ref[:, here], gift_ref[:, here]], axis=0))
        wide = dot(both, f_hi, 1, 0)
        q = wide[:RANK] + wide[RANK:] + dot(p_hi, f_lo, 1, 0)
        for j in range(tiles):
            out_ref[slot, j * RANK : (j + 1) * RANK, :] = q[:, j * LANES : (j + 1) * LANES]
        out_ref[slot, tiles * RANK :, :] = gram


def right_terms(p_sum, own, gift, replicas, slots):
    height = own.shape[1] // slots // LANES * RANK + 8
    return pl.pallas_call(
        functools.partial(right_kernel, replicas),
        in_specs=[WHOLE] * 3,
        out_specs=WHOLE,
        out_shape=jax.ShapeDtypeStruct((slots, height, LANES), F32),
        compiler_params=PARAMS,
        name="right_terms",
    )(p_sum, own, gift)


def factor_kernel(sum_ref, out_ref):
    gram = unpack(sum_ref[sum_ref.shape[0] - 8 :, :])
    row = lax.broadcasted_iota(jnp.int32, (RANK, RANK), 0)
    column = lax.broadcasted_iota(jnp.int32, (RANK, RANK), 1)
    work = jnp.concatenate([gram, (row == column).astype(F32)], axis=1)
    below = lax.broadcasted_iota(jnp.int32, (RANK, 2 * RANK), 0)
    scale = jnp.zeros((RANK, 1), F32)
    first = lax.broadcasted_iota(jnp.int32, (RANK, 1), 0)
    for k in range(RANK):
        top = work[k : k + 1, :]
        pivot = work[k : k + 1, k : k + 1]
        scale = jnp.where(first == k, lax.rsqrt(pivot), scale)
        if k < RANK - 1:
            ratio = work[:, k : k + 1] * (1.0 / pivot)
            work = jnp.where(below > k, work - ratio * top, work)
    out_ref[...] = pack(work[:, RANK:] * scale)


def inverse_factor(total):
    return pl.pallas_call(
        factor_kernel,
        in_specs=[WHOLE],
        out_specs=WHOLE,
        out_shape=jax.ShapeDtypeStruct((8, LANES), F32),
        compiler_params=PARAMS,
        cost_estimate=pl.CostEstimate(flops=4_000_000, bytes_accessed=4_000_000, transcendentals=64),
        name="inverse_factor",
    )(total)


def hat_kernel(replicas, p_ref, inverse_ref, own_ref, other_ref):
    core = lax.axis_index("c")
    inverse = unpack(inverse_ref[...])
    for place, out_ref in ((core, own_ref), (1 - core, other_ref)):
        p = unpack_rows(p_ref[place]) * (1.0 / replicas)
        out_ref[...] = pack_rows(dot(p, inverse, 1, 1, lax.Precision.HIGHEST))


def orthonormal(p_sum, inverse, replicas):
    half = jax.ShapeDtypeStruct(p_sum.shape[1:], F32)
    return pl.pallas_call(
        functools.partial(hat_kernel, replicas),
        in_specs=[WHOLE] * 2,
        out_specs=[WHOLE] * 2,
        out_shape=[half, half],
        compiler_params=PARAMS,
        cost_estimate=pl.CostEstimate(flops=4_000_000, bytes_accessed=1_000_000, transcendentals=64),
        name="orthonormal",
    )(p_sum, inverse)


def side_kernel(replicas, own_ref, other_ref, hat_ref, rows_ref):
    rows = hat_ref.shape[1]
    at = lax.broadcasted_iota(jnp.int32, (16, rows), 0) + lax.axis_index(("z", "y")) * (rows // replicas)
    chosen = (lax.broadcasted_iota(jnp.int32, (16, rows), 1) == at).astype(F32)
    for i, ref in enumerate((own_ref, other_ref)):
        hat = unpack_rows(ref[...])
        hat_ref[i] = left_three(hat)
        rows_ref[i] = left_three(dot(chosen, hat, 1, 0, lax.Precision.HIGHEST))


def left_sides(own, other, replicas):
    rows = 4 * own.shape[0]
    return pl.pallas_call(
        functools.partial(side_kernel, replicas),
        in_specs=[WHOLE] * 2,
        out_specs=[WHOLE] * 2,
        out_shape=[jax.ShapeDtypeStruct((2, rows, 3 * RANK), BF16), jax.ShapeDtypeStruct((2, 16, 3 * RANK), BF16)],
        compiler_params=PARAMS,
        cost_estimate=pl.CostEstimate(flops=4_000_000, bytes_accessed=1_000_000, transcendentals=64),
        name="left_sides",
    )(own, other)


def piece_kernel(replicas, a_ref, b_ref, inverse_ref, out_ref):
    inverse = unpack(inverse_ref[...]) * (1.0 / replicas)
    tiles = a_ref.shape[0] // RANK
    rows = a_ref[...] + b_ref[...]
    wide = jnp.concatenate([rows[j * RANK : (j + 1) * RANK] for j in range(tiles)], axis=1)
    q = dot(inverse, wide, 1, 0, lax.Precision.HIGHEST)
    for j in range(tiles):
        out_ref[j * RANK : (j + 1) * RANK, :] = q[:, j * LANES : (j + 1) * LANES]


def finished_piece(a, b, inverse, replicas):
    return pl.pallas_call(
        functools.partial(piece_kernel, replicas),
        in_specs=[WHOLE] * 3,
        out_specs=WHOLE,
        out_shape=jax.ShapeDtypeStruct(a.shape, F32),
        compiler_params=PARAMS,
        name="finished_piece",
    )(a, b, inverse)


def update_kernel(mine, pieces_ref, hat_ref, rows_ref, full_ref, m1_ref, m2_ref, *refs):
    err_hbm, n1_hbm, n2_hbm, up_hbm, q_hbm, err_ref, n1_ref, n2_ref, up_ref, q_ref, tile_ref, flat_ref, err_sem, sem = refs[-14:]
    slots, height, _ = pieces_ref.shape
    tiles = height // RANK
    width = tiles * LANES
    x = lax.axis_index("x")
    i, m = (0, lane()) if mine else (1, 1 - lane())
    copies = []
    for slot in range(slots):
        block = x ^ slot
        here = pl.ds(pl.multiple_of(block * width, width), width)
        q = jnp.concatenate([pieces_ref[slot, j * RANK : (j + 1) * RANK, :] for j in range(tiles)], axis=1)
        right = right_three(q)
        err_ref[slot] = full_ref[:, here] - dot(hat_ref[i], right, 1, 0)
        copies.append(pltpu.make_async_copy(err_ref.at[slot], err_hbm.at[0, m, :, here], err_sem.at[slot]))
        copies[-1].start()
        q_ref[:, here] = q
        state = dot(rows_ref[i], right, 1, 0)
        for j in range(tiles):
            tile_ref[block * tiles + j] = state[:8, j * LANES : (j + 1) * LANES]
    share = flat_ref.shape[0]
    for j in range(slots * tiles):
        flat_ref[:, j, :] = tile_ref[j, :share, :]
    flat = flat_ref[...].reshape(share * slots * tiles, LANES)
    n1 = 0.9 * m1_ref[m] + 0.1 * flat
    n2 = 0.95 * m2_ref[m] + 0.05 * flat * flat
    n1_ref[...] = n1
    n2_ref[...] = n2
    up_ref[...] = (n1 / (jnp.sqrt(n2) + 1e-08)).astype(BF16)
    for k, (here, there) in enumerate(((n1_ref, n1_hbm), (n2_ref, n2_hbm), (up_ref, up_hbm), (q_ref, q_hbm))):
        copies.append(pltpu.make_async_copy(here, there.at[m], sem.at[k]))
        copies[-1].start()
    for copy in copies:
        copy.wait()


def update(pieces, hat, rows, full, moment1, moment2, mine, before=()):
    depth, columns = full.shape
    projections, slots = hat.shape[0], pieces.shape[0]
    state, tiles = moment1.shape[1], columns // LANES
    return pl.pallas_call(
        functools.partial(update_kernel, mine),
        in_specs=[WHOLE] * 6 + [AWAY] * len(before),
        out_specs=[AWAY] * 5,
        out_shape=[
            pltpu.HBM((1, projections, depth, columns), F32),
            pltpu.HBM(moment1.shape, F32),
            pltpu.HBM(moment2.shape, F32),
            pltpu.HBM(moment1.shape, BF16),
            pltpu.HBM((projections, RANK, columns), F32),
        ],
        scratch_shapes=[
            pltpu.VMEM((slots, depth, columns // slots), F32),
            pltpu.VMEM((state, LANES), F32),
            pltpu.VMEM((state, LANES), F32),
            pltpu.VMEM((state, LANES), BF16),
            pltpu.VMEM((RANK, columns), F32),
            pltpu.VMEM((tiles, 8, LANES), F32),
            pltpu.VMEM((state // tiles, tiles, LANES), F32),
            pltpu.SemaphoreType.DMA((slots,)),
            pltpu.SemaphoreType.DMA((4,)),
        ],
        input_output_aliases={6 + k: k for k in range(len(before))},
        compiler_params=PARAMS,
        cost_estimate=pl.CostEstimate(flops=100_000_000, bytes_accessed=4_000_000, transcendentals=30_000),
        name="update_own" if mine else "update_other",
    )(pieces, hat, rows, full, moment1, moment2, *before)


def swap(value, axis, bit):
    names = ("z", "y", "x", "c")
    sizes = tuple(lax.axis_size(name) for name in names)
    pairs = []
    for here in np.ndindex(*sizes):
        there = list(here)
        there[names.index(axis)] ^= bit
        if axis != "c":
            there[-1] ^= bit // 2 % 2
        pairs.append((int(np.ravel_multi_index(here, sizes)), int(np.ravel_multi_index(there, sizes))))
    return lax.ppermute(value, names, pairs)


def four(values, axis):
    return (values[0] + swap(values[1], axis, 1)) + (swap(values[2], axis, 2) + swap(values[3], axis, 3))


def shards(grads, errors, q_prev, moment1, moment2):
    replicas, slots = lax.axis_size(("z", "y")), lax.axis_size("x")
    other_full, own_full, p_send, p_keep = left_factors(grads, errors, q_prev)
    p = p_keep + swap(p_send, "c", 1)
    p, other_full = lax.optimization_barrier((p, other_full))
    gift = swap(other_full, "c", 1)
    p = four([p] * 4, "y")
    p = four([p] * 4, "z")
    p = p + swap(p, "z", 6)

    terms = right_terms(p, own_full, gift, replicas, slots)
    total = four([terms[i] for i in range(slots)], "x")
    inverse = inverse_factor(total)
    q = four([total[:-8]] * 4, "y")
    q, inverse = lax.optimization_barrier((q, inverse))
    hat_own, hat_other = orthonormal(p, inverse, replicas)
    hat_gift = swap(hat_other, "c", 1)
    q = four([q] * 4, "z")
    q, hat_own, hat_gift = lax.optimization_barrier((q, hat_own, hat_gift))
    hat, rows = left_sides(hat_own, hat_gift, replicas)
    far, hat, rows = lax.optimization_barrier((swap(q, "z", 6), hat, rows))
    piece = finished_piece(q, far, inverse, replicas)
    own = jnp.stack([piece] + [swap(piece, "x", i) for i in range(1, slots)])
    other = swap(own, "c", 1)
    done = update(own, hat, rows, own_full, moment1, moment2, True)
    return tuple(update(other, hat, rows, other_full, moment1, moment2, False, done))


def solution(mesh):
    mesh = Mesh(mesh.devices.reshape(8, 4, 4, 2), ("z", "y", "x", "c"))
    dp, fsdp = ("z", "y"), ("x", "c")
    blocks = P(dp, None, fsdp, None)
    states = P(None, fsdp + dp, None)
    return jax.shard_map(
        shards,
        mesh=mesh,
        in_specs=(blocks, blocks, P(), states, states),
        out_specs=(blocks, states, states, states, P()),
        check_vma=False,
    )
```

```python
import functools

import jax
import jax.numpy as jnp
from jax import lax
from jax.experimental import pallas as pl
from jax.experimental.pallas import tpu as pltpu
from jax.sharding import Mesh, PartitionSpec as P

F32 = jnp.float32
BF16 = jnp.bfloat16
RANK = 32
LANES = 128
VMEM_LIMIT = 24 * 2**20
PARAMS = pltpu.CompilerParams(vmem_limit_bytes=VMEM_LIMIT)
WHOLE = pl.BlockSpec(memory_space=pltpu.VMEM)
AWAY = pl.BlockSpec(memory_space=pl.ANY)


def in_hbm(x):
    return pltpu.with_memory_space_constraint(x, pltpu.HBM)


def split(x):
    head = x.astype(BF16)
    return head, (x - head.astype(F32)).astype(BF16)


def left_three(x):
    hi, lo = split(x)
    return jnp.concatenate([hi, lo, hi], axis=1)


def right_three(x):
    hi, lo = split(x)
    return jnp.concatenate([hi, hi, lo], axis=0)


def dot(a, b, a_dim, b_dim, precision=None):
    return lax.dot_general(a, b, (((a_dim,), (b_dim,)), ((), ())), precision=precision, preferred_element_type=F32)


def pack(square):
    return jnp.concatenate([square[8 * i : 8 * i + 8] for i in range(4)], axis=1)


def unpack(packed):
    return jnp.concatenate([packed[:, 32 * i : 32 * i + 32] for i in range(4)], axis=0)


def pack_rows(columns):
    rows = columns.shape[0] // 4
    return jnp.concatenate([columns[rows * i : rows * (i + 1)] for i in range(4)], axis=1)


def unpack_rows(packed):
    return jnp.concatenate([packed[:, RANK * i : RANK * (i + 1)] for i in range(4)], axis=0)


def left_terms(full, q):
    q_hi, q_lo = split(q)
    f_hi, f_lo = split(full)
    wide = dot(f_hi, jnp.concatenate([q_hi, q_lo], axis=0), 1, 1)
    return pack_rows(wide[:, :RANK] + wide[:, RANK:] + dot(f_lo, q_hi, 1, 1))


def load_kernel(grads_hbm, errors_hbm, q_hbm, other_ref, p_ref, grads_ref, errors_ref, q_ref, other_grads_ref, other_q_ref, grads_sem, errors_sem, q_sem):
    core = lax.axis_index("c")
    copies = []
    for i, (m, q, grads, errors) in enumerate(((1 - core, other_q_ref, other_grads_ref, other_ref), (core, q_ref, grads_ref, errors_ref))):
        copies += [
            pltpu.make_async_copy(q_hbm.at[m], q, q_sem.at[i]),
            pltpu.make_async_copy(grads_hbm.at[0, m], grads, grads_sem.at[i]),
            pltpu.make_async_copy(errors_hbm.at[0, m], errors, errors_sem.at[i]),
        ]
    for copy in copies:
        copy.start()
    for copy in copies[:3]:
        copy.wait()
    full = other_grads_ref[...].astype(F32) + other_ref[...]
    other_ref[...] = full
    p_ref[...] = left_terms(full, other_q_ref[...])
    for copy in copies[3:]:
        copy.wait()


def load(grads, errors, q_prev):
    _, projections, rows, columns = grads.shape
    return pl.pallas_call(
        load_kernel,
        in_specs=[AWAY] * 3,
        out_specs=[WHOLE] * 5,
        out_shape=[
            pltpu.VMEM((rows, columns), F32),
            pltpu.VMEM((rows // 4, LANES), F32),
            pltpu.VMEM((rows, columns), BF16),
            pltpu.VMEM((rows, columns), F32),
            pltpu.VMEM(q_prev.shape[1:], F32),
        ],
        scratch_shapes=[
            pltpu.VMEM((rows, columns), BF16),
            pltpu.VMEM(q_prev.shape[1:], F32),
            pltpu.SemaphoreType.DMA((projections,)),
            pltpu.SemaphoreType.DMA((projections,)),
            pltpu.SemaphoreType.DMA((projections,)),
        ],
        compiler_params=PARAMS,
        name="load",
    )(in_hbm(grads), in_hbm(errors), in_hbm(q_prev))


def left_kernel(grads_ref, errors_ref, q_ref, full_ref, p_ref):
    full = grads_ref[...].astype(F32) + errors_ref[...]
    full_ref[...] = full
    p_ref[...] = left_terms(full, q_ref[...])


def left_own(grads, errors, q):
    rows, columns = grads.shape
    return pl.pallas_call(
        left_kernel,
        in_specs=[WHOLE] * 3,
        out_specs=[WHOLE] * 2,
        out_shape=[pltpu.VMEM((rows, columns), F32), pltpu.VMEM((rows // 4, LANES), F32)],
        compiler_params=PARAMS,
        cost_estimate=pl.CostEstimate(flops=100_000_000, bytes_accessed=3_000_000, transcendentals=0),
        name="left_own",
    )(grads, errors, q)


def halves_kernel(own_ref, gift_ref, hi_ref, lo_ref):
    rows = own_ref.shape[0]
    for i, ref in enumerate((own_ref, gift_ref)):
        hi, lo = split(ref[...])
        hi_ref[rows * i : rows * (i + 1)] = hi
        lo_ref[rows * i : rows * (i + 1)] = lo


def halves(own, gift):
    both = pltpu.VMEM((2 * own.shape[0], own.shape[1]), BF16)
    return pl.pallas_call(
        halves_kernel,
        in_specs=[WHOLE] * 2,
        out_specs=[WHOLE] * 2,
        out_shape=[both, both],
        compiler_params=PARAMS,
        cost_estimate=pl.CostEstimate(flops=4_000_000, bytes_accessed=3_000_000, transcendentals=0),
        name="halves",
    )(own, gift)


def right_kernel(replicas, p_ref, hi_ref, lo_ref, out_ref):
    slots, height, _ = out_ref.shape
    tiles = (height - 8) // RANK
    width = tiles * LANES
    x = lax.axis_index("x")
    half = p_ref.shape[0] // 2
    columns = jnp.concatenate([unpack_rows(p_ref[:half]), unpack_rows(p_ref[half:])], axis=0)
    p = (columns * (1.0 / replicas)).T
    p_hi, p_lo = split(p)
    both = jnp.concatenate([p_hi, p_lo], axis=0)
    gram = pack(dot(p, p, 1, 1, lax.Precision.HIGHEST))
    for slot in range(slots):
        here = pl.ds(pl.multiple_of((x ^ slot) * width, width), width)
        wide = dot(both, hi_ref[:, here], 1, 0)
        q = wide[:RANK] + wide[RANK:] + dot(p_hi, lo_ref[:, here], 1, 0)
        for j in range(tiles):
            out_ref[slot, j * RANK : (j + 1) * RANK, :] = q[:, j * LANES : (j + 1) * LANES]
        out_ref[slot, tiles * RANK :, :] = gram


def right_terms(p_sum, hi, lo, replicas, slots):
    height = hi.shape[1] // slots // LANES * RANK + 8
    return pl.pallas_call(
        functools.partial(right_kernel, replicas),
        in_specs=[WHOLE] * 3,
        out_specs=WHOLE,
        out_shape=jax.ShapeDtypeStruct((slots, height, LANES), F32),
        compiler_params=PARAMS,
        name="right_terms",
    )(p_sum, hi, lo)


def factor_kernel(sum_ref, out_ref):
    gram = unpack(sum_ref[sum_ref.shape[0] - 8 :, :])
    row = lax.broadcasted_iota(jnp.int32, (RANK, RANK), 0)
    column = lax.broadcasted_iota(jnp.int32, (RANK, RANK), 1)
    work = jnp.concatenate([gram, (row == column).astype(F32)], axis=1)
    below = lax.broadcasted_iota(jnp.int32, (RANK, 2 * RANK), 0)
    scale = jnp.zeros((RANK, 1), F32)
    first = lax.broadcasted_iota(jnp.int32, (RANK, 1), 0)
    for k in range(RANK):
        top = work[k : k + 1, :]
        pivot = work[k : k + 1, k : k + 1]
        scale = jnp.where(first == k, lax.rsqrt(pivot), scale)
        if k < RANK - 1:
            ratio = work[:, k : k + 1] * (1.0 / pivot)
            work = jnp.where(below > k, work - ratio * top, work)
    out_ref[...] = pack(work[:, RANK:] * scale)


def inverse_factor(total):
    return pl.pallas_call(
        factor_kernel,
        in_specs=[WHOLE],
        out_specs=WHOLE,
        out_shape=jax.ShapeDtypeStruct((8, LANES), F32),
        compiler_params=PARAMS,
        cost_estimate=pl.CostEstimate(flops=4_000_000, bytes_accessed=4_000_000, transcendentals=64),
        name="inverse_factor",
    )(total)


def hat_kernel(replicas, p_ref, inverse_ref, own_ref, other_ref):
    half = p_ref.shape[0] // 2
    inverse = unpack(inverse_ref[...])
    for i, out_ref in enumerate((own_ref, other_ref)):
        p = unpack_rows(p_ref[half * i : half * (i + 1)]) * (1.0 / replicas)
        out_ref[...] = pack_rows(dot(p, inverse, 1, 1, lax.Precision.HIGHEST))


def orthonormal(p_sum, inverse, replicas):
    half = jax.ShapeDtypeStruct((p_sum.shape[0] // 2, LANES), F32)
    return pl.pallas_call(
        functools.partial(hat_kernel, replicas),
        in_specs=[WHOLE] * 2,
        out_specs=[WHOLE] * 2,
        out_shape=[half, half],
        compiler_params=PARAMS,
        cost_estimate=pl.CostEstimate(flops=4_000_000, bytes_accessed=1_000_000, transcendentals=64),
        name="orthonormal",
    )(p_sum, inverse)


def side_kernel(replicas, own_ref, other_ref, hat_ref, rows_ref):
    rows = hat_ref.shape[1]
    at = lax.broadcasted_iota(jnp.int32, (16, rows), 0) + lax.axis_index(("z", "y")) * (rows // replicas)
    chosen = (lax.broadcasted_iota(jnp.int32, (16, rows), 1) == at).astype(F32)
    for i, ref in enumerate((own_ref, other_ref)):
        hat = unpack_rows(ref[...])
        hat_ref[i] = left_three(hat)
        rows_ref[i] = left_three(dot(chosen, hat, 1, 0, lax.Precision.HIGHEST))


def left_sides(own, other, replicas):
    rows = 4 * own.shape[0]
    return pl.pallas_call(
        functools.partial(side_kernel, replicas),
        in_specs=[WHOLE] * 2,
        out_specs=[WHOLE] * 2,
        out_shape=[jax.ShapeDtypeStruct((2, rows, 3 * RANK), BF16), jax.ShapeDtypeStruct((2, 16, 3 * RANK), BF16)],
        compiler_params=PARAMS,
        cost_estimate=pl.CostEstimate(flops=4_000_000, bytes_accessed=1_000_000, transcendentals=64),
        name="left_sides",
    )(own, other)


def piece_kernel(replicas, a_ref, b_ref, inverse_ref, out_ref):
    inverse = unpack(inverse_ref[...]) * (1.0 / replicas)
    tiles = a_ref.shape[0] // RANK
    rows = a_ref[...] + b_ref[...]
    wide = jnp.concatenate([rows[j * RANK : (j + 1) * RANK] for j in range(tiles)], axis=1)
    q = dot(inverse, wide, 1, 0, lax.Precision.HIGHEST)
    for j in range(tiles):
        out_ref[j * RANK : (j + 1) * RANK, :] = q[:, j * LANES : (j + 1) * LANES]


def finished_piece(a, b, inverse, replicas):
    return pl.pallas_call(
        functools.partial(piece_kernel, replicas),
        in_specs=[WHOLE] * 3,
        out_specs=WHOLE,
        out_shape=jax.ShapeDtypeStruct(a.shape, F32),
        compiler_params=PARAMS,
        name="finished_piece",
    )(a, b, inverse)


def update_kernel(mine, pieces_ref, hat_ref, rows_ref, full_ref, m1_ref, m2_ref, *refs):
    err_hbm, n1_hbm, n2_hbm, up_hbm, q_hbm, err_ref, n1_ref, n2_ref, up_ref, q_ref, tile_ref, flat_ref, err_sem, sem = refs[-14:]
    slots, height, _ = pieces_ref.shape
    tiles = height // RANK
    width = tiles * LANES
    x, core = lax.axis_index("x"), lax.axis_index("c")
    i, m = (0, core) if mine else (1, 1 - core)
    copies = []
    for slot in range(slots):
        block = x ^ slot
        here = pl.ds(pl.multiple_of(block * width, width), width)
        q = jnp.concatenate([pieces_ref[slot, j * RANK : (j + 1) * RANK, :] for j in range(tiles)], axis=1)
        right = right_three(q)
        err_ref[slot] = full_ref[:, here] - dot(hat_ref[i], right, 1, 0)
        copies.append(pltpu.make_async_copy(err_ref.at[slot], err_hbm.at[0, m, :, here], err_sem.at[slot]))
        copies[-1].start()
        q_ref[:, here] = q
        state = dot(rows_ref[i], right, 1, 0)
        for j in range(tiles):
            tile_ref[block * tiles + j] = state[:8, j * LANES : (j + 1) * LANES]
    share = flat_ref.shape[0]
    for j in range(slots * tiles):
        flat_ref[:, j, :] = tile_ref[j, :share, :]
    flat = flat_ref[...].reshape(share * slots * tiles, LANES)
    n1 = 0.9 * m1_ref[m] + 0.1 * flat
    n2 = 0.95 * m2_ref[m] + 0.05 * flat * flat
    n1_ref[...] = n1
    n2_ref[...] = n2
    up_ref[...] = (n1 / (jnp.sqrt(n2) + 1e-08)).astype(BF16)
    for k, (here, there) in enumerate(((n1_ref, n1_hbm), (n2_ref, n2_hbm), (up_ref, up_hbm), (q_ref, q_hbm))):
        copies.append(pltpu.make_async_copy(here, there.at[m], sem.at[k]))
        copies[-1].start()
    for copy in copies:
        copy.wait()


def update(pieces, hat, rows, full, moment1, moment2, mine, before=()):
    depth, columns = full.shape
    projections, slots = hat.shape[0], pieces.shape[0]
    state, tiles = moment1.shape[1], columns // LANES
    return pl.pallas_call(
        functools.partial(update_kernel, mine),
        in_specs=[WHOLE] * 6 + [AWAY] * len(before),
        out_specs=[AWAY] * 5,
        out_shape=[
            pltpu.HBM((1, projections, depth, columns), F32),
            pltpu.HBM(moment1.shape, F32),
            pltpu.HBM(moment2.shape, F32),
            pltpu.HBM(moment1.shape, BF16),
            pltpu.HBM((projections, RANK, columns), F32),
        ],
        scratch_shapes=[
            pltpu.VMEM((slots, depth, columns // slots), F32),
            pltpu.VMEM((state, LANES), F32),
            pltpu.VMEM((state, LANES), F32),
            pltpu.VMEM((state, LANES), BF16),
            pltpu.VMEM((RANK, columns), F32),
            pltpu.VMEM((tiles, 8, LANES), F32),
            pltpu.VMEM((state // tiles, tiles, LANES), F32),
            pltpu.SemaphoreType.DMA((slots,)),
            pltpu.SemaphoreType.DMA((4,)),
        ],
        input_output_aliases={6 + k: k for k in range(len(before))},
        compiler_params=PARAMS,
        cost_estimate=pl.CostEstimate(flops=100_000_000, bytes_accessed=4_000_000, transcendentals=30_000),
        name="update_own" if mine else "update_other",
    )(pieces, hat, rows, full, moment1, moment2, *before)


def swap(value, axis, bit):
    return lax.ppermute(value, axis, [(i, i ^ bit) for i in range(lax.axis_size(axis))])


def four(values, axis):
    return (values[0] + swap(values[1], axis, 1)) + (swap(values[2], axis, 2) + swap(values[3], axis, 3))


def shards(grads, errors, q_prev, moment1, moment2):
    replicas, slots = lax.axis_size(("z", "y")), lax.axis_size("x")
    other_full, p_other, own_grads, own_errors, own_q = load(grads, errors, q_prev)
    own_full, p_own = left_own(own_grads, own_errors, own_q)
    p = jnp.concatenate([p_own, swap(p_other, "c", 1)])
    p, gift = lax.optimization_barrier((p, other_full))
    gift = swap(gift, "c", 1)
    p = four([p] * 4, "y")
    p = four([p] * 4, "z")
    far, hi, lo = lax.optimization_barrier((swap(p, "z", 6), *halves(own_full, gift)))
    p = p + far

    terms = right_terms(p, hi, lo, replicas, slots)
    total = four([terms[i] for i in range(slots)], "x")
    inverse = inverse_factor(total)
    q = four([total[:-8]] * 4, "y")
    q, inverse = lax.optimization_barrier((q, inverse))
    hat_own, hat_other = orthonormal(p, inverse, replicas)
    hat_gift = swap(hat_other, "c", 1)
    q = four([q] * 4, "z")
    q, hat_own, hat_gift = lax.optimization_barrier((q, hat_own, hat_gift))
    hat, rows = left_sides(hat_own, hat_gift, replicas)
    far, hat, rows = lax.optimization_barrier((swap(q, "z", 6), hat, rows))
    piece = finished_piece(q, far, inverse, replicas)
    own = jnp.stack([piece] + [swap(piece, "x", i) for i in range(1, slots)])
    other = swap(own, "c", 1)
    done = update(own, hat, rows, own_full, moment1, moment2, True)
    return tuple(update(other, hat, rows, other_full, moment1, moment2, False, done))


def solution(mesh):
    mesh = Mesh(mesh.devices.reshape(8, 4, 4, 2), ("z", "y", "x", "c"))
    dp, fsdp = ("z", "y"), ("x", "c")
    blocks = P(dp, None, fsdp, None)
    states = P(None, fsdp + dp, None)
    return jax.shard_map(
        shards,
        mesh=mesh,
        in_specs=(blocks, blocks, P(), states, states),
        out_specs=(blocks, states, states, states, P()),
        check_vma=False,
    )
```

```python
import functools

import jax
import jax.numpy as jnp
from jax import lax
from jax.experimental import pallas as pl
from jax.experimental.pallas import tpu as pltpu
from jax.sharding import Mesh, PartitionSpec as P

F32 = jnp.float32
BF16 = jnp.bfloat16
RANK = 32
LANES = 128
VMEM_LIMIT = 24 * 2**20
PARAMS = pltpu.CompilerParams(vmem_limit_bytes=VMEM_LIMIT)
WHOLE = pl.BlockSpec(memory_space=pltpu.VMEM)
AWAY = pl.BlockSpec(memory_space=pl.ANY)


def in_hbm(x):
    return pltpu.with_memory_space_constraint(x, pltpu.HBM)


def split(x):
    head = x.astype(BF16)
    return head, (x - head.astype(F32)).astype(BF16)


def left_three(x):
    hi, lo = split(x)
    return jnp.concatenate([hi, lo, hi], axis=1)


def right_three(x):
    hi, lo = split(x)
    return jnp.concatenate([hi, hi, lo], axis=0)


def dot(a, b, a_dim, b_dim, precision=None):
    return lax.dot_general(a, b, (((a_dim,), (b_dim,)), ((), ())), precision=precision, preferred_element_type=F32)


def pack(square):
    return jnp.concatenate([square[8 * i : 8 * i + 8] for i in range(4)], axis=1)


def unpack(packed):
    return jnp.concatenate([packed[:, 32 * i : 32 * i + 32] for i in range(4)], axis=0)


def pack_rows(columns):
    rows = columns.shape[0] // 4
    return jnp.concatenate([columns[rows * i : rows * (i + 1)] for i in range(4)], axis=1)


def unpack_rows(packed):
    return jnp.concatenate([packed[:, RANK * i : RANK * (i + 1)] for i in range(4)], axis=0)


def left_terms(full, q):
    q_hi, q_lo = split(q)
    f_hi, f_lo = split(full)
    wide = dot(f_hi, jnp.concatenate([q_hi, q_lo], axis=0), 1, 1)
    return pack_rows(wide[:, :RANK] + wide[:, RANK:] + dot(f_lo, q_hi, 1, 1))


def load_kernel(grads_hbm, errors_hbm, q_hbm, other_ref, p_ref, grads_ref, errors_ref, q_ref, other_grads_ref, other_q_ref, grads_sem, errors_sem, q_sem):
    core = lax.axis_index("c")
    copies = []
    for i, (m, q, grads, errors) in enumerate(((1 - core, other_q_ref, other_grads_ref, other_ref), (core, q_ref, grads_ref, errors_ref))):
        copies += [
            pltpu.make_async_copy(q_hbm.at[m], q, q_sem.at[i]),
            pltpu.make_async_copy(grads_hbm.at[0, m], grads, grads_sem.at[i]),
            pltpu.make_async_copy(errors_hbm.at[0, m], errors, errors_sem.at[i]),
        ]
    for copy in copies:
        copy.start()
    for copy in copies[:3]:
        copy.wait()
    full = other_grads_ref[...].astype(F32) + other_ref[...]
    other_ref[...] = full
    p_ref[...] = left_terms(full, other_q_ref[...])
    for copy in copies[3:]:
        copy.wait()


def load(grads, errors, q_prev):
    _, projections, rows, columns = grads.shape
    return pl.pallas_call(
        load_kernel,
        in_specs=[AWAY] * 3,
        out_specs=[WHOLE] * 5,
        out_shape=[
            pltpu.VMEM((rows, columns), F32),
            pltpu.VMEM((rows // 4, LANES), F32),
            pltpu.VMEM((rows, columns), BF16),
            pltpu.VMEM((rows, columns), F32),
            pltpu.VMEM(q_prev.shape[1:], F32),
        ],
        scratch_shapes=[
            pltpu.VMEM((rows, columns), BF16),
            pltpu.VMEM(q_prev.shape[1:], F32),
            pltpu.SemaphoreType.DMA((projections,)),
            pltpu.SemaphoreType.DMA((projections,)),
            pltpu.SemaphoreType.DMA((projections,)),
        ],
        compiler_params=PARAMS,
        name="load",
    )(in_hbm(grads), in_hbm(errors), in_hbm(q_prev))


def left_kernel(grads_ref, errors_ref, q_ref, full_ref, p_ref):
    full = grads_ref[...].astype(F32) + errors_ref[...]
    full_ref[...] = full
    p_ref[...] = left_terms(full, q_ref[...])


def left_own(grads, errors, q):
    rows, columns = grads.shape
    return pl.pallas_call(
        left_kernel,
        in_specs=[WHOLE] * 3,
        out_specs=[WHOLE] * 2,
        out_shape=[pltpu.VMEM((rows, columns), F32), pltpu.VMEM((rows // 4, LANES), F32)],
        compiler_params=PARAMS,
        cost_estimate=pl.CostEstimate(flops=100_000_000, bytes_accessed=3_000_000, transcendentals=0),
        name="left_own",
    )(grads, errors, q)


def halves_kernel(own_ref, gift_ref, hi_ref, lo_ref):
    rows = own_ref.shape[0]
    for i, ref in enumerate((own_ref, gift_ref)):
        hi, lo = split(ref[...])
        hi_ref[rows * i : rows * (i + 1)] = hi
        lo_ref[rows * i : rows * (i + 1)] = lo


def halves(own, gift):
    both = pltpu.VMEM((2 * own.shape[0], own.shape[1]), BF16)
    return pl.pallas_call(
        halves_kernel,
        in_specs=[WHOLE] * 2,
        out_specs=[WHOLE] * 2,
        out_shape=[both, both],
        compiler_params=PARAMS,
        cost_estimate=pl.CostEstimate(flops=4_000_000, bytes_accessed=3_000_000, transcendentals=0),
        name="halves",
    )(own, gift)


def right_kernel(replicas, p_ref, hi_ref, lo_ref, out_ref):
    slots, height, _ = out_ref.shape
    tiles = (height - 8) // RANK
    width = tiles * LANES
    x = lax.axis_index("x")
    half = p_ref.shape[0] // 2
    columns = jnp.concatenate([unpack_rows(p_ref[:half]), unpack_rows(p_ref[half:])], axis=0)
    p = (columns * (1.0 / replicas)).T
    p_hi, p_lo = split(p)
    both = jnp.concatenate([p_hi, p_lo], axis=0)
    gram = pack(dot(p, p, 1, 1, lax.Precision.HIGHEST))
    for slot in range(slots):
        here = pl.ds(pl.multiple_of((x ^ slot) * width, width), width)
        wide = dot(both, hi_ref[:, here], 1, 0)
        q = wide[:RANK] + wide[RANK:] + dot(p_hi, lo_ref[:, here], 1, 0)
        for j in range(tiles):
            out_ref[slot, j * RANK : (j + 1) * RANK, :] = q[:, j * LANES : (j + 1) * LANES]
        out_ref[slot, tiles * RANK :, :] = gram


def right_terms(p_sum, hi, lo, replicas, slots):
    height = hi.shape[1] // slots // LANES * RANK + 8
    return pl.pallas_call(
        functools.partial(right_kernel, replicas),
        in_specs=[WHOLE] * 3,
        out_specs=WHOLE,
        out_shape=jax.ShapeDtypeStruct((slots, height, LANES), F32),
        compiler_params=PARAMS,
        name="right_terms",
    )(p_sum, hi, lo)


def factor_kernel(sum_ref, out_ref):
    gram = unpack(sum_ref[sum_ref.shape[0] - 8 :, :])
    row = lax.broadcasted_iota(jnp.int32, (RANK, RANK), 0)
    column = lax.broadcasted_iota(jnp.int32, (RANK, RANK), 1)
    work = jnp.concatenate([gram, (row == column).astype(F32)], axis=1)
    below = lax.broadcasted_iota(jnp.int32, (RANK, 2 * RANK), 0)
    scale = jnp.zeros((RANK, 1), F32)
    first = lax.broadcasted_iota(jnp.int32, (RANK, 1), 0)
    for k in range(RANK):
        top = work[k : k + 1, :]
        pivot = work[k : k + 1, k : k + 1]
        scale = jnp.where(first == k, lax.rsqrt(pivot), scale)
        if k < RANK - 1:
            ratio = work[:, k : k + 1] * (1.0 / pivot)
            work = jnp.where(below > k, work - ratio * top, work)
    out_ref[...] = pack(work[:, RANK:] * scale)


def inverse_factor(total):
    return pl.pallas_call(
        factor_kernel,
        in_specs=[WHOLE],
        out_specs=WHOLE,
        out_shape=jax.ShapeDtypeStruct((8, LANES), F32),
        compiler_params=PARAMS,
        cost_estimate=pl.CostEstimate(flops=4_000_000, bytes_accessed=4_000_000, transcendentals=64),
        name="inverse_factor",
    )(total)


def hat_kernel(replicas, p_ref, inverse_ref, own_ref, other_ref):
    half = p_ref.shape[0] // 2
    inverse = unpack(inverse_ref[...])
    for i, out_ref in enumerate((own_ref, other_ref)):
        p = unpack_rows(p_ref[half * i : half * (i + 1)]) * (1.0 / replicas)
        out_ref[...] = pack_rows(dot(p, inverse, 1, 1, lax.Precision.HIGHEST))


def orthonormal(p_sum, inverse, replicas):
    half = jax.ShapeDtypeStruct((p_sum.shape[0] // 2, LANES), F32)
    return pl.pallas_call(
        functools.partial(hat_kernel, replicas),
        in_specs=[WHOLE] * 2,
        out_specs=[WHOLE] * 2,
        out_shape=[half, half],
        compiler_params=PARAMS,
        cost_estimate=pl.CostEstimate(flops=4_000_000, bytes_accessed=1_000_000, transcendentals=64),
        name="orthonormal",
    )(p_sum, inverse)


def side_kernel(replicas, own_ref, other_ref, hat_ref, rows_ref):
    rows = hat_ref.shape[1]
    at = lax.broadcasted_iota(jnp.int32, (16, rows), 0) + lax.axis_index(("z", "y")) * (rows // replicas)
    chosen = (lax.broadcasted_iota(jnp.int32, (16, rows), 1) == at).astype(F32)
    for i, ref in enumerate((own_ref, other_ref)):
        hat = unpack_rows(ref[...])
        hat_ref[i] = left_three(hat)
        rows_ref[i] = left_three(dot(chosen, hat, 1, 0, lax.Precision.HIGHEST))


def left_sides(own, other, replicas):
    rows = 4 * own.shape[0]
    return pl.pallas_call(
        functools.partial(side_kernel, replicas),
        in_specs=[WHOLE] * 2,
        out_specs=[WHOLE] * 2,
        out_shape=[jax.ShapeDtypeStruct((2, rows, 3 * RANK), BF16), jax.ShapeDtypeStruct((2, 16, 3 * RANK), BF16)],
        compiler_params=PARAMS,
        cost_estimate=pl.CostEstimate(flops=4_000_000, bytes_accessed=1_000_000, transcendentals=64),
        name="left_sides",
    )(own, other)


def piece_kernel(replicas, a_ref, b_ref, inverse_ref, out_ref):
    inverse = unpack(inverse_ref[...]) * (1.0 / replicas)
    tiles = a_ref.shape[0] // RANK
    rows = a_ref[...] + b_ref[...]
    wide = jnp.concatenate([rows[j * RANK : (j + 1) * RANK] for j in range(tiles)], axis=1)
    q = dot(inverse, wide, 1, 0, lax.Precision.HIGHEST)
    for j in range(tiles):
        out_ref[j * RANK : (j + 1) * RANK, :] = q[:, j * LANES : (j + 1) * LANES]


def finished_piece(a, b, inverse, replicas):
    return pl.pallas_call(
        functools.partial(piece_kernel, replicas),
        in_specs=[WHOLE] * 3,
        out_specs=WHOLE,
        out_shape=jax.ShapeDtypeStruct(a.shape, F32),
        compiler_params=PARAMS,
        name="finished_piece",
    )(a, b, inverse)


def update_kernel(counts, blocks, adam, *refs):
    names = ("pieces", "hat", "rows", "full", "moments", "before", "out", "scratch")
    groups = {}
    for name, count in zip(names, counts, strict=True):
        groups[name], refs = refs[:count], refs[count:]
    (hat_ref,), (rows_ref,) = groups["hat"], groups["rows"]
    err_hbm = groups["out"][0]
    err_ref, err_sem = groups["scratch"][:2]
    x, own = lax.axis_index("x"), lax.axis_index("c")
    depth, width = err_ref.shape[1:]
    tiles = width // LANES

    def piece(array, index):
        ref = groups["pieces"][array]
        return jnp.concatenate([ref[index, j * RANK : (j + 1) * RANK, :] for j in range(tiles)], axis=1)

    def place(slot):
        return pl.ds(pl.multiple_of((x ^ slot) * width, width), width)

    copies = []

    def send(here, there, sem):
        copies.append(pltpu.make_async_copy(here, there, sem))
        copies[-1].start()

    for k, (i, slot, array, index) in enumerate(blocks):
        right = right_three(piece(array, index))
        err_ref[k] = groups["full"][i][:, place(slot)] - dot(hat_ref[i], right, 1, 0)
        send(err_ref.at[k], err_hbm.at[0, (own + i) % 2, :, place(slot)], err_sem.at[k])
    if adam is not None:
        i, sources = adam
        m = (own + i) % 2
        m1_ref, m2_ref = groups["moments"]
        n1_ref, n2_ref, up_ref, q_ref, tile_ref, flat_ref, sem = groups["scratch"][2:]
        for slot, (array, index) in enumerate(sources):
            q = piece(array, index)
            q_ref[:, place(slot)] = q
            state = dot(rows_ref[i], right_three(q), 1, 0)
            for j in range(tiles):
                tile_ref[(x ^ slot) * tiles + j] = state[:8, j * LANES : (j + 1) * LANES]
        share, total = flat_ref.shape[:2]
        for j in range(total):
            flat_ref[:, j, :] = tile_ref[j, :share, :]
        flat = flat_ref[...].reshape(share * total, LANES)
        n1 = 0.9 * m1_ref[m] + 0.1 * flat
        n2 = 0.95 * m2_ref[m] + 0.05 * flat * flat
        n1_ref[...] = n1
        n2_ref[...] = n2
        up_ref[...] = (n1 / (jnp.sqrt(n2) + 1e-08)).astype(BF16)
        for k, (here, there) in enumerate(zip((n1_ref, n2_ref, up_ref, q_ref), groups["out"][1:], strict=True)):
            send(here, there.at[m], sem.at[k])
    for copy in copies:
        copy.wait()


def update(blocks, adam, hat, rows, fulls, moments, name, before=()):
    arrays = []

    def at(pieces):
        for k, array in enumerate(arrays):
            if array is pieces:
                return k
        arrays.append(pieces)
        return len(arrays) - 1

    blocks = tuple((i, slot, at(pieces), index) for i, slot, pieces, index in blocks)
    if adam is not None:
        adam = (adam[0], tuple((at(pieces), index) for pieces, index in adam[1]))
    depth, columns = fulls[0].shape
    state, tiles = moments[0].shape[1], columns // LANES
    width = arrays[0].shape[1] // RANK * LANES
    out = [pltpu.HBM((1, 2, depth, columns), F32)]
    scratch = [pltpu.VMEM((len(blocks), depth, width), F32), pltpu.SemaphoreType.DMA((len(blocks),))]
    if adam is None:
        moments = ()
    else:
        shape = moments[0].shape
        out += [pltpu.HBM(shape, F32), pltpu.HBM(shape, F32), pltpu.HBM(shape, BF16), pltpu.HBM((2, RANK, columns), F32)]
        scratch += [
            pltpu.VMEM((state, LANES), F32),
            pltpu.VMEM((state, LANES), F32),
            pltpu.VMEM((state, LANES), BF16),
            pltpu.VMEM((RANK, columns), F32),
            pltpu.VMEM((tiles, 8, LANES), F32),
            pltpu.VMEM((state // tiles, tiles, LANES), F32),
            pltpu.SemaphoreType.DMA((4,)),
        ]
    given = (*arrays, hat, rows, *fulls, *moments)
    counts = (len(arrays), 1, 1, len(fulls), len(moments), len(before), len(out), len(scratch))
    return pl.pallas_call(
        functools.partial(update_kernel, counts, blocks, adam),
        in_specs=[WHOLE] * len(given) + [AWAY] * len(before),
        out_specs=[AWAY] * len(out),
        out_shape=out,
        scratch_shapes=scratch,
        input_output_aliases={len(given) + k: k for k in range(len(before))},
        compiler_params=PARAMS,
        cost_estimate=pl.CostEstimate(flops=20_000_000 * len(blocks), bytes_accessed=1_000_000 * len(blocks), transcendentals=30_000),
        name=name,
    )(*given, *before)


def swap(value, axis, bit):
    return lax.ppermute(value, axis, [(i, i ^ bit) for i in range(lax.axis_size(axis))])


def four(values, axis):
    return (values[0] + swap(values[1], axis, 1)) + (swap(values[2], axis, 2) + swap(values[3], axis, 3))


def shards(grads, errors, q_prev, moment1, moment2):
    replicas, slots = lax.axis_size(("z", "y")), lax.axis_size("x")
    other_full, p_other, own_grads, own_errors, own_q = load(grads, errors, q_prev)
    own_full, p_own = left_own(own_grads, own_errors, own_q)
    p = jnp.concatenate([p_own, swap(p_other, "c", 1)])
    p, gift = lax.optimization_barrier((p, other_full))
    gift = swap(gift, "c", 1)
    p = four([p] * 4, "y")
    p = four([p] * 4, "z")
    far, hi, lo = lax.optimization_barrier((swap(p, "z", 6), *halves(own_full, gift)))
    p = p + far

    terms = right_terms(p, hi, lo, replicas, slots)
    total = four([terms[i] for i in range(slots)], "x")
    inverse = inverse_factor(total)
    q = four([total[:-8]] * 4, "y")
    q, inverse = lax.optimization_barrier((q, inverse))
    hat_own, hat_other = orthonormal(p, inverse, replicas)
    hat_gift = swap(hat_other, "c", 1)
    q = four([q] * 4, "z")
    q, hat_own, hat_gift = lax.optimization_barrier((q, hat_own, hat_gift))
    hat, rows = left_sides(hat_own, hat_gift, replicas)
    far, hat, rows = lax.optimization_barrier((swap(q, "z", 6), hat, rows))
    piece = finished_piece(q, far, inverse, replicas)
    side = (hat, rows, (own_full, other_full), (moment1, moment2))
    own0 = piece[None]
    other0 = swap(own0, "c", 1)
    own3, own2, own1 = (swap(own0, "x", i) for i in (3, 2, 1))
    other3 = swap(own3, "c", 1)
    err = update([(0, 0, own0, 0), (1, 0, other0, 0)], None, *side, "update_first")
    err = update([(0, 3, own3, 0)], None, *side, "update_second", err)
    own1, own2, other3, err = lax.optimization_barrier((own1, own2, other3, err))
    last = swap(jnp.concatenate([own1, own2]), "c", 1)
    sources = [(own0, 0), (own1, 0), (own2, 0), (own3, 0)]
    done = update([(0, 1, own1, 0), (0, 2, own2, 0), (1, 3, other3, 0)], (0, sources), *side, "update_third", err)
    sources = [(other0, 0), (last, 0), (last, 1), (other3, 0)]
    return tuple(update([(1, 1, last, 0), (1, 2, last, 1)], (1, sources), *side, "update_fourth", done))


def solution(mesh):
    mesh = Mesh(mesh.devices.reshape(8, 4, 4, 2), ("z", "y", "x", "c"))
    dp, fsdp = ("z", "y"), ("x", "c")
    blocks = P(dp, None, fsdp, None)
    states = P(None, fsdp + dp, None)
    return jax.shard_map(
        shards,
        mesh=mesh,
        in_specs=(blocks, blocks, P(), states, states),
        out_specs=(blocks, states, states, states, P()),
        check_vma=False,
    )
```

```python
import functools

import jax
import jax.numpy as jnp
from jax import lax
from jax.experimental import pallas as pl
from jax.experimental.pallas import tpu as pltpu
from jax.sharding import Mesh, PartitionSpec as P

F32 = jnp.float32
BF16 = jnp.bfloat16
RANK = 32
LANES = 128
VMEM_LIMIT = 24 * 2**20
PARAMS = pltpu.CompilerParams(vmem_limit_bytes=VMEM_LIMIT)
WHOLE = pl.BlockSpec(memory_space=pltpu.VMEM)
AWAY = pl.BlockSpec(memory_space=pl.ANY)


def in_hbm(x):
    return pltpu.with_memory_space_constraint(x, pltpu.HBM)


def split(x):
    head = x.astype(BF16)
    return head, (x - head.astype(F32)).astype(BF16)


def left_three(x):
    hi, lo = split(x)
    return jnp.concatenate([hi, lo, hi], axis=1)


def right_three(x):
    hi, lo = split(x)
    return jnp.concatenate([hi, hi, lo], axis=0)


def dot(a, b, a_dim, b_dim, precision=None):
    return lax.dot_general(a, b, (((a_dim,), (b_dim,)), ((), ())), precision=precision, preferred_element_type=F32)


def pack(square):
    return jnp.concatenate([square[8 * i : 8 * i + 8] for i in range(4)], axis=1)


def unpack(packed):
    return jnp.concatenate([packed[:, 32 * i : 32 * i + 32] for i in range(4)], axis=0)


def pack_rows(columns):
    rows = columns.shape[0] // 4
    return jnp.concatenate([columns[rows * i : rows * (i + 1)] for i in range(4)], axis=1)


def unpack_rows(packed):
    return jnp.concatenate([packed[:, RANK * i : RANK * (i + 1)] for i in range(4)], axis=0)


def left_terms(full, q):
    q_hi, q_lo = split(q)
    f_hi, f_lo = split(full)
    wide = dot(f_hi, jnp.concatenate([q_hi, q_lo], axis=0), 1, 1)
    return pack_rows(wide[:, :RANK] + wide[:, RANK:] + dot(f_lo, q_hi, 1, 1))


def load_kernel(grads_hbm, errors_hbm, q_hbm, other_ref, p_ref, grads_ref, errors_ref, q_ref, other_grads_ref, other_q_ref, grads_sem, errors_sem, q_sem):
    core = lax.axis_index("c")
    copies = []
    for i, (m, q, grads, errors) in enumerate(((1 - core, other_q_ref, other_grads_ref, other_ref), (core, q_ref, grads_ref, errors_ref))):
        copies += [
            pltpu.make_async_copy(q_hbm.at[m], q, q_sem.at[i]),
            pltpu.make_async_copy(grads_hbm.at[0, m], grads, grads_sem.at[i]),
            pltpu.make_async_copy(errors_hbm.at[0, m], errors, errors_sem.at[i]),
        ]
    for copy in copies:
        copy.start()
    for copy in copies[:3]:
        copy.wait()
    full = other_grads_ref[...].astype(F32) + other_ref[...]
    other_ref[...] = full
    p_ref[...] = left_terms(full, other_q_ref[...])
    for copy in copies[3:]:
        copy.wait()


def load(grads, errors, q_prev):
    _, projections, rows, columns = grads.shape
    return pl.pallas_call(
        load_kernel,
        in_specs=[AWAY] * 3,
        out_specs=[WHOLE] * 5,
        out_shape=[
            pltpu.VMEM((rows, columns), F32),
            pltpu.VMEM((rows // 4, LANES), F32),
            pltpu.VMEM((rows, columns), BF16),
            pltpu.VMEM((rows, columns), F32),
            pltpu.VMEM(q_prev.shape[1:], F32),
        ],
        scratch_shapes=[
            pltpu.VMEM((rows, columns), BF16),
            pltpu.VMEM(q_prev.shape[1:], F32),
            pltpu.SemaphoreType.DMA((projections,)),
            pltpu.SemaphoreType.DMA((projections,)),
            pltpu.SemaphoreType.DMA((projections,)),
        ],
        compiler_params=PARAMS,
        name="load",
    )(in_hbm(grads), in_hbm(errors), in_hbm(q_prev))


def left_kernel(grads_ref, errors_ref, q_ref, full_ref, p_ref):
    full = grads_ref[...].astype(F32) + errors_ref[...]
    full_ref[...] = full
    p_ref[...] = left_terms(full, q_ref[...])


def left_own(grads, errors, q):
    rows, columns = grads.shape
    return pl.pallas_call(
        left_kernel,
        in_specs=[WHOLE] * 3,
        out_specs=[WHOLE] * 2,
        out_shape=[pltpu.VMEM((rows, columns), F32), pltpu.VMEM((rows // 4, LANES), F32)],
        compiler_params=PARAMS,
        cost_estimate=pl.CostEstimate(flops=100_000_000, bytes_accessed=3_000_000, transcendentals=0),
        name="left_own",
    )(grads, errors, q)


def halves_kernel(own_ref, gift_ref, hi_ref, lo_ref):
    rows = own_ref.shape[0]
    for i, ref in enumerate((own_ref, gift_ref)):
        hi, lo = split(ref[...])
        hi_ref[rows * i : rows * (i + 1)] = hi
        lo_ref[rows * i : rows * (i + 1)] = lo


def halves(own, gift):
    both = pltpu.VMEM((2 * own.shape[0], own.shape[1]), BF16)
    return pl.pallas_call(
        halves_kernel,
        in_specs=[WHOLE] * 2,
        out_specs=[WHOLE] * 2,
        out_shape=[both, both],
        compiler_params=PARAMS,
        cost_estimate=pl.CostEstimate(flops=4_000_000, bytes_accessed=3_000_000, transcendentals=0),
        name="halves",
    )(own, gift)


def right_kernel(replicas, slots, p_ref, hi_ref, lo_ref, out_ref):
    height = out_ref.shape[1]
    tiles = (height - 8) // RANK
    width = tiles * LANES
    x = lax.axis_index("x")
    half = p_ref.shape[0] // 2
    columns = jnp.concatenate([unpack_rows(p_ref[:half]), unpack_rows(p_ref[half:])], axis=0)
    p = (columns * (1.0 / replicas)).T
    p_hi, p_lo = split(p)
    both = jnp.concatenate([p_hi, p_lo], axis=0)
    gram = pack(dot(p, p, 1, 1, lax.Precision.HIGHEST))
    for k, slot in enumerate(slots):
        here = pl.ds(pl.multiple_of((x ^ slot) * width, width), width)
        wide = dot(both, hi_ref[:, here], 1, 0)
        q = wide[:RANK] + wide[RANK:] + dot(p_hi, lo_ref[:, here], 1, 0)
        for j in range(tiles):
            out_ref[k, j * RANK : (j + 1) * RANK, :] = q[:, j * LANES : (j + 1) * LANES]
        out_ref[k, tiles * RANK :, :] = gram


def right_terms(p_sum, hi, lo, replicas, slots, total):
    height = hi.shape[1] // total // LANES * RANK + 8
    return pl.pallas_call(
        functools.partial(right_kernel, replicas, slots),
        in_specs=[WHOLE] * 3,
        out_specs=WHOLE,
        out_shape=jax.ShapeDtypeStruct((len(slots), height, LANES), F32),
        compiler_params=PARAMS,
        cost_estimate=pl.CostEstimate(flops=200_000_000, bytes_accessed=2_000_000, transcendentals=0),
        name="right_terms_kept" if slots == (0,) else "right_terms_sent",
    )(p_sum, hi, lo)


def factor_kernel(sum_ref, out_ref):
    gram = unpack(sum_ref[sum_ref.shape[0] - 8 :, :])
    row = lax.broadcasted_iota(jnp.int32, (RANK, RANK), 0)
    column = lax.broadcasted_iota(jnp.int32, (RANK, RANK), 1)
    work = jnp.concatenate([gram, (row == column).astype(F32)], axis=1)
    below = lax.broadcasted_iota(jnp.int32, (RANK, 2 * RANK), 0)
    scale = jnp.zeros((RANK, 1), F32)
    first = lax.broadcasted_iota(jnp.int32, (RANK, 1), 0)
    for k in range(RANK):
        top = work[k : k + 1, :]
        pivot = work[k : k + 1, k : k + 1]
        scale = jnp.where(first == k, lax.rsqrt(pivot), scale)
        if k < RANK - 1:
            ratio = work[:, k : k + 1] * (1.0 / pivot)
            work = jnp.where(below > k, work - ratio * top, work)
    out_ref[...] = pack(work[:, RANK:] * scale)


def inverse_factor(total):
    return pl.pallas_call(
        factor_kernel,
        in_specs=[WHOLE],
        out_specs=WHOLE,
        out_shape=jax.ShapeDtypeStruct((8, LANES), F32),
        compiler_params=PARAMS,
        cost_estimate=pl.CostEstimate(flops=4_000_000, bytes_accessed=4_000_000, transcendentals=64),
        name="inverse_factor",
    )(total)


def hat_kernel(replicas, p_ref, inverse_ref, own_ref, other_ref):
    half = p_ref.shape[0] // 2
    inverse = unpack(inverse_ref[...])
    for i, out_ref in enumerate((own_ref, other_ref)):
        p = unpack_rows(p_ref[half * i : half * (i + 1)]) * (1.0 / replicas)
        out_ref[...] = pack_rows(dot(p, inverse, 1, 1, lax.Precision.HIGHEST))


def orthonormal(p_sum, inverse, replicas):
    half = jax.ShapeDtypeStruct((p_sum.shape[0] // 2, LANES), F32)
    return pl.pallas_call(
        functools.partial(hat_kernel, replicas),
        in_specs=[WHOLE] * 2,
        out_specs=[WHOLE] * 2,
        out_shape=[half, half],
        compiler_params=PARAMS,
        cost_estimate=pl.CostEstimate(flops=4_000_000, bytes_accessed=1_000_000, transcendentals=64),
        name="orthonormal",
    )(p_sum, inverse)


def side_kernel(replicas, own_ref, other_ref, hat_ref, rows_ref):
    rows = hat_ref.shape[1]
    at = lax.broadcasted_iota(jnp.int32, (16, rows), 0) + lax.axis_index(("z", "y")) * (rows // replicas)
    chosen = (lax.broadcasted_iota(jnp.int32, (16, rows), 1) == at).astype(F32)
    for i, ref in enumerate((own_ref, other_ref)):
        hat = unpack_rows(ref[...])
        hat_ref[i] = left_three(hat)
        rows_ref[i] = left_three(dot(chosen, hat, 1, 0, lax.Precision.HIGHEST))


def left_sides(own, other, replicas):
    rows = 4 * own.shape[0]
    return pl.pallas_call(
        functools.partial(side_kernel, replicas),
        in_specs=[WHOLE] * 2,
        out_specs=[WHOLE] * 2,
        out_shape=[jax.ShapeDtypeStruct((2, rows, 3 * RANK), BF16), jax.ShapeDtypeStruct((2, 16, 3 * RANK), BF16)],
        compiler_params=PARAMS,
        cost_estimate=pl.CostEstimate(flops=4_000_000, bytes_accessed=1_000_000, transcendentals=64),
        name="left_sides",
    )(own, other)


def piece_kernel(replicas, a_ref, b_ref, inverse_ref, out_ref):
    inverse = unpack(inverse_ref[...]) * (1.0 / replicas)
    tiles = a_ref.shape[0] // RANK
    rows = a_ref[...] + b_ref[...]
    wide = jnp.concatenate([rows[j * RANK : (j + 1) * RANK] for j in range(tiles)], axis=1)
    q = dot(inverse, wide, 1, 0, lax.Precision.HIGHEST)
    for j in range(tiles):
        out_ref[j * RANK : (j + 1) * RANK, :] = q[:, j * LANES : (j + 1) * LANES]


def finished_piece(a, b, inverse, replicas):
    return pl.pallas_call(
        functools.partial(piece_kernel, replicas),
        in_specs=[WHOLE] * 3,
        out_specs=WHOLE,
        out_shape=jax.ShapeDtypeStruct(a.shape, F32),
        compiler_params=PARAMS,
        name="finished_piece",
    )(a, b, inverse)


def update_kernel(mine, pieces_ref, hat_ref, rows_ref, full_ref, m1_ref, m2_ref, *refs):
    err_hbm, n1_hbm, n2_hbm, up_hbm, q_hbm, err_ref, n1_ref, n2_ref, up_ref, q_ref, tile_ref, flat_ref, err_sem, sem = refs[-14:]
    slots, height, _ = pieces_ref.shape
    tiles = height // RANK
    width = tiles * LANES
    x, core = lax.axis_index("x"), lax.axis_index("c")
    i, m = (0, core) if mine else (1, 1 - core)
    copies = []
    for slot in range(slots):
        block = x ^ slot
        here = pl.ds(pl.multiple_of(block * width, width), width)
        q = jnp.concatenate([pieces_ref[slot, j * RANK : (j + 1) * RANK, :] for j in range(tiles)], axis=1)
        right = right_three(q)
        err_ref[slot] = full_ref[:, here] - dot(hat_ref[i], right, 1, 0)
        copies.append(pltpu.make_async_copy(err_ref.at[slot], err_hbm.at[0, m, :, here], err_sem.at[slot]))
        copies[-1].start()
        q_ref[:, here] = q
        state = dot(rows_ref[i], right, 1, 0)
        for j in range(tiles):
            tile_ref[block * tiles + j] = state[:8, j * LANES : (j + 1) * LANES]
    share = flat_ref.shape[0]
    for j in range(slots * tiles):
        flat_ref[:, j, :] = tile_ref[j, :share, :]
    flat = flat_ref[...].reshape(share * slots * tiles, LANES)
    n1 = 0.9 * m1_ref[m] + 0.1 * flat
    n2 = 0.95 * m2_ref[m] + 0.05 * flat * flat
    n1_ref[...] = n1
    n2_ref[...] = n2
    up_ref[...] = (n1 / (jnp.sqrt(n2) + 1e-08)).astype(BF16)
    for k, (here, there) in enumerate(((n1_ref, n1_hbm), (n2_ref, n2_hbm), (up_ref, up_hbm), (q_ref, q_hbm))):
        copies.append(pltpu.make_async_copy(here, there.at[m], sem.at[k]))
        copies[-1].start()
    for copy in copies:
        copy.wait()


def update(pieces, hat, rows, full, moment1, moment2, mine, before=()):
    depth, columns = full.shape
    projections, slots = hat.shape[0], pieces.shape[0]
    state, tiles = moment1.shape[1], columns // LANES
    return pl.pallas_call(
        functools.partial(update_kernel, mine),
        in_specs=[WHOLE] * 6 + [AWAY] * len(before),
        out_specs=[AWAY] * 5,
        out_shape=[
            pltpu.HBM((1, projections, depth, columns), F32),
            pltpu.HBM(moment1.shape, F32),
            pltpu.HBM(moment2.shape, F32),
            pltpu.HBM(moment1.shape, BF16),
            pltpu.HBM((projections, RANK, columns), F32),
        ],
        scratch_shapes=[
            pltpu.VMEM((slots, depth, columns // slots), F32),
            pltpu.VMEM((state, LANES), F32),
            pltpu.VMEM((state, LANES), F32),
            pltpu.VMEM((state, LANES), BF16),
            pltpu.VMEM((RANK, columns), F32),
            pltpu.VMEM((tiles, 8, LANES), F32),
            pltpu.VMEM((state // tiles, tiles, LANES), F32),
            pltpu.SemaphoreType.DMA((slots,)),
            pltpu.SemaphoreType.DMA((4,)),
        ],
        input_output_aliases={6 + k: k for k in range(len(before))},
        compiler_params=PARAMS,
        cost_estimate=pl.CostEstimate(flops=100_000_000, bytes_accessed=4_000_000, transcendentals=30_000),
        name="update_own" if mine else "update_other",
    )(pieces, hat, rows, full, moment1, moment2, *before)


def swap(value, axis, bit):
    return lax.ppermute(value, axis, [(i, i ^ bit) for i in range(lax.axis_size(axis))])


def four(values, axis):
    return (values[0] + swap(values[1], axis, 1)) + (swap(values[2], axis, 2) + swap(values[3], axis, 3))


def shards(grads, errors, q_prev, moment1, moment2):
    replicas, slots = lax.axis_size(("z", "y")), lax.axis_size("x")
    other_full, p_other, own_grads, own_errors, own_q = load(grads, errors, q_prev)
    own_full, p_own = left_own(own_grads, own_errors, own_q)
    p_own, gift = lax.optimization_barrier((p_own, other_full))
    p = jnp.concatenate([p_own, swap(p_other, "c", 1)])
    gift = swap(gift, "c", 1)
    p = four([p] * 4, "y")
    p = four([p] * 4, "z")
    far, hi, lo = lax.optimization_barrier((swap(p, "z", 6), *halves(own_full, gift)))
    p = p + far

    sent = right_terms(p, hi, lo, replicas, tuple(range(1, slots)), slots)
    kept = right_terms(p, hi, lo, replicas, (0,), slots)
    total = four([kept[0], *(sent[i - 1] for i in range(1, slots))], "x")
    inverse = inverse_factor(total)
    q = four([total[:-8]] * 4, "y")
    q, inverse = lax.optimization_barrier((q, inverse))
    hat_own, hat_other = orthonormal(p, inverse, replicas)
    hat_gift = swap(hat_other, "c", 1)
    q = four([q] * 4, "z")
    q, hat_own, hat_gift = lax.optimization_barrier((q, hat_own, hat_gift))
    hat, rows = left_sides(hat_own, hat_gift, replicas)
    far, hat, rows = lax.optimization_barrier((swap(q, "z", 6), hat, rows))
    piece = finished_piece(q, far, inverse, replicas)
    own = jnp.stack([piece] + [swap(piece, "x", i) for i in range(1, slots)])
    other = swap(own, "c", 1)
    done = update(own, hat, rows, own_full, moment1, moment2, True)
    return tuple(update(other, hat, rows, other_full, moment1, moment2, False, done))


def solution(mesh):
    mesh = Mesh(mesh.devices.reshape(8, 4, 4, 2), ("z", "y", "x", "c"))
    dp, fsdp = ("z", "y"), ("x", "c")
    blocks = P(dp, None, fsdp, None)
    states = P(None, fsdp + dp, None)
    return jax.shard_map(
        shards,
        mesh=mesh,
        in_specs=(blocks, blocks, P(), states, states),
        out_specs=(blocks, states, states, states, P()),
        check_vma=False,
    )
```

```python
import functools

import jax
import jax.numpy as jnp
from jax import lax
from jax.experimental import pallas as pl
from jax.experimental.pallas import tpu as pltpu
from jax.sharding import Mesh, PartitionSpec as P

F32 = jnp.float32
BF16 = jnp.bfloat16
RANK = 32
LANES = 128
VMEM_LIMIT = 24 * 2**20
PARAMS = pltpu.CompilerParams(vmem_limit_bytes=VMEM_LIMIT)
WHOLE = pl.BlockSpec(memory_space=pltpu.VMEM)
AWAY = pl.BlockSpec(memory_space=pl.ANY)


def in_hbm(x):
    return pltpu.with_memory_space_constraint(x, pltpu.HBM)


def split(x):
    head = x.astype(BF16)
    return head, (x - head.astype(F32)).astype(BF16)


def left_three(x):
    hi, lo = split(x)
    return jnp.concatenate([hi, lo, hi], axis=1)


def right_three(x):
    hi, lo = split(x)
    return jnp.concatenate([hi, hi, lo], axis=0)


def dot(a, b, a_dim, b_dim, precision=None):
    return lax.dot_general(a, b, (((a_dim,), (b_dim,)), ((), ())), precision=precision, preferred_element_type=F32)


def pack(square):
    return jnp.concatenate([square[8 * i : 8 * i + 8] for i in range(4)], axis=1)


def unpack(packed):
    return jnp.concatenate([packed[:, 32 * i : 32 * i + 32] for i in range(4)], axis=0)


def pack_rows(columns):
    rows = columns.shape[0] // 4
    return jnp.concatenate([columns[rows * i : rows * (i + 1)] for i in range(4)], axis=1)


def unpack_rows(packed):
    return jnp.concatenate([packed[:, RANK * i : RANK * (i + 1)] for i in range(4)], axis=0)


def left_terms(full, q):
    q_hi, q_lo = split(q)
    f_hi, f_lo = split(full)
    wide = dot(f_hi, jnp.concatenate([q_hi, q_lo], axis=0), 1, 1)
    return pack_rows(wide[:, :RANK] + wide[:, RANK:] + dot(f_lo, q_hi, 1, 1))


def load_kernel(grads_hbm, errors_hbm, q_hbm, other_ref, p_ref, grads_ref, errors_ref, q_ref, other_grads_ref, other_q_ref, grads_sem, errors_sem, q_sem):
    core = lax.axis_index("c")
    copies = []
    for i, (m, q, grads, errors) in enumerate(((1 - core, other_q_ref, other_grads_ref, other_ref), (core, q_ref, grads_ref, errors_ref))):
        copies += [
            pltpu.make_async_copy(q_hbm.at[m], q, q_sem.at[i]),
            pltpu.make_async_copy(grads_hbm.at[0, m], grads, grads_sem.at[i]),
            pltpu.make_async_copy(errors_hbm.at[0, m], errors, errors_sem.at[i]),
        ]
    for copy in copies:
        copy.start()
    for copy in copies[:3]:
        copy.wait()
    full = other_grads_ref[...].astype(F32) + other_ref[...]
    other_ref[...] = full
    p_ref[...] = left_terms(full, other_q_ref[...])
    for copy in copies[3:]:
        copy.wait()


def load(grads, errors, q_prev):
    _, projections, rows, columns = grads.shape
    return pl.pallas_call(
        load_kernel,
        in_specs=[AWAY] * 3,
        out_specs=[WHOLE] * 5,
        out_shape=[
            pltpu.VMEM((rows, columns), F32),
            pltpu.VMEM((rows // 4, LANES), F32),
            pltpu.VMEM((rows, columns), BF16),
            pltpu.VMEM((rows, columns), F32),
            pltpu.VMEM(q_prev.shape[1:], F32),
        ],
        scratch_shapes=[
            pltpu.VMEM((rows, columns), BF16),
            pltpu.VMEM(q_prev.shape[1:], F32),
            pltpu.SemaphoreType.DMA((projections,)),
            pltpu.SemaphoreType.DMA((projections,)),
            pltpu.SemaphoreType.DMA((projections,)),
        ],
        compiler_params=PARAMS,
        name="load",
    )(in_hbm(grads), in_hbm(errors), in_hbm(q_prev))


def left_kernel(grads_ref, errors_ref, q_ref, full_ref, p_ref):
    full = grads_ref[...].astype(F32) + errors_ref[...]
    full_ref[...] = full
    p_ref[...] = left_terms(full, q_ref[...])


def left_own(grads, errors, q):
    rows, columns = grads.shape
    return pl.pallas_call(
        left_kernel,
        in_specs=[WHOLE] * 3,
        out_specs=[WHOLE] * 2,
        out_shape=[pltpu.VMEM((rows, columns), F32), pltpu.VMEM((rows // 4, LANES), F32)],
        compiler_params=PARAMS,
        cost_estimate=pl.CostEstimate(flops=100_000_000, bytes_accessed=3_000_000, transcendentals=0),
        name="left_own",
    )(grads, errors, q)


def halves_kernel(own_ref, gift_ref, hi_ref, lo_ref):
    rows = own_ref.shape[0]
    for i, ref in enumerate((own_ref, gift_ref)):
        hi, lo = split(ref[...])
        hi_ref[rows * i : rows * (i + 1)] = hi
        lo_ref[rows * i : rows * (i + 1)] = lo


def halves(own, gift):
    both = pltpu.VMEM((2 * own.shape[0], own.shape[1]), BF16)
    return pl.pallas_call(
        halves_kernel,
        in_specs=[WHOLE] * 2,
        out_specs=[WHOLE] * 2,
        out_shape=[both, both],
        compiler_params=PARAMS,
        cost_estimate=pl.CostEstimate(flops=4_000_000, bytes_accessed=3_000_000, transcendentals=0),
        name="halves",
    )(own, gift)


def right_kernel(replicas, p_ref, hi_ref, lo_ref, out_ref):
    slots, height, _ = out_ref.shape
    tiles = (height - 8) // RANK
    width = tiles * LANES
    x = lax.axis_index("x")
    half = p_ref.shape[0] // 2
    columns = jnp.concatenate([unpack_rows(p_ref[:half]), unpack_rows(p_ref[half:])], axis=0)
    p = (columns * (1.0 / replicas)).T
    p_hi, p_lo = split(p)
    both = jnp.concatenate([p_hi, p_lo], axis=0)
    gram = pack(dot(p, p, 1, 1, lax.Precision.HIGHEST))
    for slot in range(slots):
        here = pl.ds(pl.multiple_of((x ^ slot) * width, width), width)
        wide = dot(both, hi_ref[:, here], 1, 0)
        q = wide[:RANK] + wide[RANK:] + dot(p_hi, lo_ref[:, here], 1, 0)
        for j in range(tiles):
            out_ref[slot, j * RANK : (j + 1) * RANK, :] = q[:, j * LANES : (j + 1) * LANES]
        out_ref[slot, tiles * RANK :, :] = gram


def right_terms(p_sum, hi, lo, replicas, slots):
    height = hi.shape[1] // slots // LANES * RANK + 8
    return pl.pallas_call(
        functools.partial(right_kernel, replicas),
        in_specs=[WHOLE] * 3,
        out_specs=WHOLE,
        out_shape=jax.ShapeDtypeStruct((slots, height, LANES), F32),
        compiler_params=PARAMS,
        name="right_terms",
    )(p_sum, hi, lo)


def factor_kernel(sum_ref, out_ref):
    gram = unpack(sum_ref[sum_ref.shape[0] - 8 :, :])
    row = lax.broadcasted_iota(jnp.int32, (RANK, RANK), 0)
    column = lax.broadcasted_iota(jnp.int32, (RANK, RANK), 1)
    work = jnp.concatenate([gram, (row == column).astype(F32)], axis=1)
    below = lax.broadcasted_iota(jnp.int32, (RANK, 2 * RANK), 0)
    scale = jnp.zeros((RANK, 1), F32)
    first = lax.broadcasted_iota(jnp.int32, (RANK, 1), 0)
    for k in range(RANK):
        top = work[k : k + 1, :]
        pivot = work[k : k + 1, k : k + 1]
        scale = jnp.where(first == k, lax.rsqrt(pivot), scale)
        if k < RANK - 1:
            ratio = work[:, k : k + 1] * (1.0 / pivot)
            work = jnp.where(below > k, work - ratio * top, work)
    out_ref[...] = pack(work[:, RANK:] * scale)


def inverse_factor(total):
    return pl.pallas_call(
        factor_kernel,
        in_specs=[WHOLE],
        out_specs=WHOLE,
        out_shape=jax.ShapeDtypeStruct((8, LANES), F32),
        compiler_params=PARAMS,
        cost_estimate=pl.CostEstimate(flops=4_000_000, bytes_accessed=4_000_000, transcendentals=64),
        name="inverse_factor",
    )(total)


def hat_kernel(replicas, p_ref, inverse_ref, own_ref, other_ref):
    half = p_ref.shape[0] // 2
    inverse = unpack(inverse_ref[...])
    for i, out_ref in enumerate((own_ref, other_ref)):
        p = unpack_rows(p_ref[half * i : half * (i + 1)]) * (1.0 / replicas)
        out_ref[...] = pack_rows(dot(p, inverse, 1, 1, lax.Precision.HIGHEST))


def orthonormal(p_sum, inverse, replicas):
    half = jax.ShapeDtypeStruct((p_sum.shape[0] // 2, LANES), F32)
    return pl.pallas_call(
        functools.partial(hat_kernel, replicas),
        in_specs=[WHOLE] * 2,
        out_specs=[WHOLE] * 2,
        out_shape=[half, half],
        compiler_params=PARAMS,
        cost_estimate=pl.CostEstimate(flops=4_000_000, bytes_accessed=1_000_000, transcendentals=64),
        name="orthonormal",
    )(p_sum, inverse)


def side_kernel(replicas, own_ref, other_ref, hat_ref, rows_ref):
    rows = hat_ref.shape[1]
    at = lax.broadcasted_iota(jnp.int32, (16, rows), 0) + lax.axis_index(("z", "y")) * (rows // replicas)
    chosen = (lax.broadcasted_iota(jnp.int32, (16, rows), 1) == at).astype(F32)
    for i, ref in enumerate((own_ref, other_ref)):
        hat = unpack_rows(ref[...])
        hat_ref[i] = left_three(hat)
        rows_ref[i] = left_three(dot(chosen, hat, 1, 0, lax.Precision.HIGHEST))


def left_sides(own, other, replicas):
    rows = 4 * own.shape[0]
    return pl.pallas_call(
        functools.partial(side_kernel, replicas),
        in_specs=[WHOLE] * 2,
        out_specs=[WHOLE] * 2,
        out_shape=[jax.ShapeDtypeStruct((2, rows, 3 * RANK), BF16), jax.ShapeDtypeStruct((2, 16, 3 * RANK), BF16)],
        compiler_params=PARAMS,
        cost_estimate=pl.CostEstimate(flops=4_000_000, bytes_accessed=1_000_000, transcendentals=64),
        name="left_sides",
    )(own, other)


def piece_kernel(replicas, a_ref, b_ref, inverse_ref, out_ref):
    inverse = unpack(inverse_ref[...]) * (1.0 / replicas)
    tiles = a_ref.shape[0] // RANK
    rows = a_ref[...] + b_ref[...]
    wide = jnp.concatenate([rows[j * RANK : (j + 1) * RANK] for j in range(tiles)], axis=1)
    q = dot(inverse, wide, 1, 0, lax.Precision.HIGHEST)
    for j in range(tiles):
        out_ref[j * RANK : (j + 1) * RANK, :] = q[:, j * LANES : (j + 1) * LANES]


def finished_piece(a, b, inverse, replicas):
    return pl.pallas_call(
        functools.partial(piece_kernel, replicas),
        in_specs=[WHOLE] * 3,
        out_specs=WHOLE,
        out_shape=jax.ShapeDtypeStruct(a.shape, F32),
        compiler_params=PARAMS,
        name="finished_piece",
    )(a, b, inverse)


def update_kernel(counts, blocks, adam, *refs):
    names = ("pieces", "hat", "rows", "full", "moments", "before", "out", "scratch")
    groups = {}
    for name, count in zip(names, counts, strict=True):
        groups[name], refs = refs[:count], refs[count:]
    (hat_ref,), (rows_ref,) = groups["hat"], groups["rows"]
    err_hbm = groups["out"][0]
    err_ref, err_sem = groups["scratch"][:2]
    x, own = lax.axis_index("x"), lax.axis_index("c")
    depth, width = err_ref.shape[1:]
    tiles = width // LANES

    def piece(array, index):
        ref = groups["pieces"][array]
        return jnp.concatenate([ref[index, j * RANK : (j + 1) * RANK, :] for j in range(tiles)], axis=1)

    def place(slot):
        return pl.ds(pl.multiple_of((x ^ slot) * width, width), width)

    copies = []

    def send(here, there, sem):
        copies.append(pltpu.make_async_copy(here, there, sem))
        copies[-1].start()

    for k, (i, slot, array, index) in enumerate(blocks):
        right = right_three(piece(array, index))
        err_ref[k] = groups["full"][i][:, place(slot)] - dot(hat_ref[i], right, 1, 0)
        send(err_ref.at[k], err_hbm.at[0, (own + i) % 2, :, place(slot)], err_sem.at[k])
    if adam is not None:
        i, sources = adam
        m = (own + i) % 2
        m1_ref, m2_ref = groups["moments"]
        n1_ref, n2_ref, up_ref, q_ref, tile_ref, flat_ref, sem = groups["scratch"][2:]
        for slot, (array, index) in enumerate(sources):
            q = piece(array, index)
            q_ref[:, place(slot)] = q
            state = dot(rows_ref[i], right_three(q), 1, 0)
            for j in range(tiles):
                tile_ref[(x ^ slot) * tiles + j] = state[:8, j * LANES : (j + 1) * LANES]
        share, total = flat_ref.shape[:2]
        for j in range(total):
            flat_ref[:, j, :] = tile_ref[j, :share, :]
        flat = flat_ref[...].reshape(share * total, LANES)
        n1 = 0.9 * m1_ref[m] + 0.1 * flat
        n2 = 0.95 * m2_ref[m] + 0.05 * flat * flat
        n1_ref[...] = n1
        n2_ref[...] = n2
        up_ref[...] = (n1 / (jnp.sqrt(n2) + 1e-08)).astype(BF16)
        for k, (here, there) in enumerate(zip((n1_ref, n2_ref, up_ref, q_ref), groups["out"][1:], strict=True)):
            send(here, there.at[m], sem.at[k])
    for copy in copies:
        copy.wait()


def update(blocks, adam, hat, rows, fulls, moments, name, before=()):
    arrays = []

    def at(pieces):
        for k, array in enumerate(arrays):
            if array is pieces:
                return k
        arrays.append(pieces)
        return len(arrays) - 1

    blocks = tuple((i, slot, at(pieces), index) for i, slot, pieces, index in blocks)
    if adam is not None:
        adam = (adam[0], tuple((at(pieces), index) for pieces, index in adam[1]))
    depth, columns = fulls[0].shape
    state, tiles = moments[0].shape[1], columns // LANES
    width = arrays[0].shape[1] // RANK * LANES
    out = [pltpu.HBM((1, 2, depth, columns), F32)]
    scratch = [pltpu.VMEM((len(blocks), depth, width), F32), pltpu.SemaphoreType.DMA((len(blocks),))]
    if adam is None:
        moments = ()
    else:
        shape = moments[0].shape
        out += [pltpu.HBM(shape, F32), pltpu.HBM(shape, F32), pltpu.HBM(shape, BF16), pltpu.HBM((2, RANK, columns), F32)]
        scratch += [
            pltpu.VMEM((state, LANES), F32),
            pltpu.VMEM((state, LANES), F32),
            pltpu.VMEM((state, LANES), BF16),
            pltpu.VMEM((RANK, columns), F32),
            pltpu.VMEM((tiles, 8, LANES), F32),
            pltpu.VMEM((state // tiles, tiles, LANES), F32),
            pltpu.SemaphoreType.DMA((4,)),
        ]
    given = (*arrays, hat, rows, *fulls, *moments)
    counts = (len(arrays), 1, 1, len(fulls), len(moments), len(before), len(out), len(scratch))
    return pl.pallas_call(
        functools.partial(update_kernel, counts, blocks, adam),
        in_specs=[WHOLE] * len(given) + [AWAY] * len(before),
        out_specs=[AWAY] * len(out),
        out_shape=out,
        scratch_shapes=scratch,
        input_output_aliases={len(given) + k: k for k in range(len(before))},
        compiler_params=PARAMS,
        cost_estimate=pl.CostEstimate(flops=20_000_000 * len(blocks), bytes_accessed=1_000_000 * len(blocks), transcendentals=30_000),
        name=name,
    )(*given, *before)


def swap(value, axis, bit):
    return lax.ppermute(value, axis, [(i, i ^ bit) for i in range(lax.axis_size(axis))])


def four(values, axis):
    return (values[0] + swap(values[1], axis, 1)) + (swap(values[2], axis, 2) + swap(values[3], axis, 3))


def shards(grads, errors, q_prev, moment1, moment2):
    replicas, slots = lax.axis_size(("z", "y")), lax.axis_size("x")
    other_full, p_other, own_grads, own_errors, own_q = load(grads, errors, q_prev)
    own_full, p_own = left_own(own_grads, own_errors, own_q)
    p = jnp.concatenate([p_own, swap(p_other, "c", 1)])
    p, gift = lax.optimization_barrier((p, other_full))
    gift = swap(gift, "c", 1)
    p = four([p] * 4, "y")
    p = four([p] * 4, "z")
    far, hi, lo = lax.optimization_barrier((swap(p, "z", 6), *halves(own_full, gift)))
    p = p + far

    terms = right_terms(p, hi, lo, replicas, slots)
    total = four([terms[i] for i in range(slots)], "x")
    inverse = inverse_factor(total)
    q = four([total[:-8]] * 4, "y")
    q, inverse = lax.optimization_barrier((q, inverse))
    hat_own, hat_other = orthonormal(p, inverse, replicas)
    hat_gift = swap(hat_other, "c", 1)
    q = four([q] * 4, "z")
    q, hat_own, hat_gift = lax.optimization_barrier((q, hat_own, hat_gift))
    hat, rows = left_sides(hat_own, hat_gift, replicas)
    far, hat, rows = lax.optimization_barrier((swap(q, "z", 6), hat, rows))
    piece = finished_piece(q, far, inverse, replicas)
    side = (hat, rows, (own_full, other_full), (moment1, moment2))
    own0 = piece[None]
    own3, own2, own1 = (swap(own0, "x", i) for i in (3, 2, 1))
    err = update([(0, 0, own0, 0), (0, 3, own3, 0)], None, *side, "update_first")
    own1, own2, err = lax.optimization_barrier((own1, own2, err))
    last = swap(jnp.concatenate([own0, own1, own2, own3]), "c", 1)
    sources = [(own0, 0), (own1, 0), (own2, 0), (own3, 0)]
    done = update([(0, 1, own1, 0), (0, 2, own2, 0)], (0, sources), *side, "update_second", err)
    sources = [(last, i) for i in range(4)]
    blocks = [(1, i, last, i) for i in range(4)]
    return tuple(update(blocks, (1, sources), *side, "update_third", done))


def solution(mesh):
    mesh = Mesh(mesh.devices.reshape(8, 4, 4, 2), ("z", "y", "x", "c"))
    dp, fsdp = ("z", "y"), ("x", "c")
    blocks = P(dp, None, fsdp, None)
    states = P(None, fsdp + dp, None)
    return jax.shard_map(
        shards,
        mesh=mesh,
        in_specs=(blocks, blocks, P(), states, states),
        out_specs=(blocks, states, states, states, P()),
        check_vma=False,
    )
```

```python
import functools

import jax
import jax.numpy as jnp
from jax import lax
from jax.experimental import pallas as pl
from jax.experimental.pallas import tpu as pltpu
from jax.sharding import Mesh, PartitionSpec as P

F32 = jnp.float32
BF16 = jnp.bfloat16
RANK = 32
LANES = 128
VMEM_LIMIT = 24 * 2**20
PARAMS = pltpu.CompilerParams(vmem_limit_bytes=VMEM_LIMIT)
WHOLE = pl.BlockSpec(memory_space=pltpu.VMEM)
AWAY = pl.BlockSpec(memory_space=pl.ANY)


def in_hbm(x):
    return pltpu.with_memory_space_constraint(x, pltpu.HBM)


def split(x):
    head = x.astype(BF16)
    return head, (x - head.astype(F32)).astype(BF16)


def left_three(x):
    hi, lo = split(x)
    return jnp.concatenate([hi, lo, hi], axis=1)


def right_three(x):
    hi, lo = split(x)
    return jnp.concatenate([hi, hi, lo], axis=0)


def dot(a, b, a_dim, b_dim, precision=None):
    return lax.dot_general(a, b, (((a_dim,), (b_dim,)), ((), ())), precision=precision, preferred_element_type=F32)


def pack(square):
    return jnp.concatenate([square[8 * i : 8 * i + 8] for i in range(4)], axis=1)


def unpack(packed):
    return jnp.concatenate([packed[:, 32 * i : 32 * i + 32] for i in range(4)], axis=0)


def pack_rows(columns):
    rows = columns.shape[0] // 4
    return jnp.concatenate([columns[rows * i : rows * (i + 1)] for i in range(4)], axis=1)


def unpack_rows(packed):
    return jnp.concatenate([packed[:, RANK * i : RANK * (i + 1)] for i in range(4)], axis=0)


def left_terms(full, q):
    q_hi, q_lo = split(q)
    f_hi, f_lo = split(full)
    wide = dot(f_hi, jnp.concatenate([q_hi, q_lo], axis=0), 1, 1)
    return pack_rows(wide[:, :RANK] + wide[:, RANK:] + dot(f_lo, q_hi, 1, 1))


def load_kernel(grads_hbm, errors_hbm, q_hbm, other_ref, p_ref, grads_ref, errors_ref, q_ref, other_grads_ref, other_q_ref, grads_sem, errors_sem, q_sem):
    core = lax.axis_index("c")
    copies = []
    for i, (m, q, grads, errors) in enumerate(((1 - core, other_q_ref, other_grads_ref, other_ref), (core, q_ref, grads_ref, errors_ref))):
        copies += [
            pltpu.make_async_copy(q_hbm.at[m], q, q_sem.at[i]),
            pltpu.make_async_copy(grads_hbm.at[0, m], grads, grads_sem.at[i]),
            pltpu.make_async_copy(errors_hbm.at[0, m], errors, errors_sem.at[i]),
        ]
    for copy in copies:
        copy.start()
    for copy in copies[:3]:
        copy.wait()
    full = other_grads_ref[...].astype(F32) + other_ref[...]
    other_ref[...] = full
    p_ref[...] = left_terms(full, other_q_ref[...])
    for copy in copies[3:]:
        copy.wait()


def load(grads, errors, q_prev):
    _, projections, rows, columns = grads.shape
    return pl.pallas_call(
        load_kernel,
        in_specs=[AWAY] * 3,
        out_specs=[WHOLE] * 5,
        out_shape=[
            pltpu.VMEM((rows, columns), F32),
            pltpu.VMEM((rows // 4, LANES), F32),
            pltpu.VMEM((rows, columns), BF16),
            pltpu.VMEM((rows, columns), F32),
            pltpu.VMEM(q_prev.shape[1:], F32),
        ],
        scratch_shapes=[
            pltpu.VMEM((rows, columns), BF16),
            pltpu.VMEM(q_prev.shape[1:], F32),
            pltpu.SemaphoreType.DMA((projections,)),
            pltpu.SemaphoreType.DMA((projections,)),
            pltpu.SemaphoreType.DMA((projections,)),
        ],
        compiler_params=PARAMS,
        name="load",
    )(in_hbm(grads), in_hbm(errors), in_hbm(q_prev))


def left_kernel(grads_ref, errors_ref, q_ref, full_ref, p_ref):
    full = grads_ref[...].astype(F32) + errors_ref[...]
    full_ref[...] = full
    p_ref[...] = left_terms(full, q_ref[...])


def left_own(grads, errors, q):
    rows, columns = grads.shape
    return pl.pallas_call(
        left_kernel,
        in_specs=[WHOLE] * 3,
        out_specs=[WHOLE] * 2,
        out_shape=[pltpu.VMEM((rows, columns), F32), pltpu.VMEM((rows // 4, LANES), F32)],
        compiler_params=PARAMS,
        cost_estimate=pl.CostEstimate(flops=100_000_000, bytes_accessed=3_000_000, transcendentals=0),
        name="left_own",
    )(grads, errors, q)


def halves_kernel(own_ref, gift_ref, hi_ref, lo_ref):
    rows = own_ref.shape[0]
    for i, ref in enumerate((own_ref, gift_ref)):
        hi, lo = split(ref[...])
        hi_ref[rows * i : rows * (i + 1)] = hi
        lo_ref[rows * i : rows * (i + 1)] = lo


def halves(own, gift):
    both = pltpu.VMEM((2 * own.shape[0], own.shape[1]), BF16)
    return pl.pallas_call(
        halves_kernel,
        in_specs=[WHOLE] * 2,
        out_specs=[WHOLE] * 2,
        out_shape=[both, both],
        compiler_params=PARAMS,
        cost_estimate=pl.CostEstimate(flops=4_000_000, bytes_accessed=3_000_000, transcendentals=0),
        name="halves",
    )(own, gift)


def right_kernel(replicas, p_ref, hi_ref, lo_ref, out_ref):
    slots, height, _ = out_ref.shape
    tiles = (height - 8) // RANK
    width = tiles * LANES
    x = lax.axis_index("x")
    half = p_ref.shape[0] // 2
    columns = jnp.concatenate([unpack_rows(p_ref[:half]), unpack_rows(p_ref[half:])], axis=0)
    p = (columns * (1.0 / replicas)).T
    p_hi, p_lo = split(p)
    both = jnp.concatenate([p_hi, p_lo], axis=0)
    gram = pack(dot(p, p, 1, 1, lax.Precision.HIGHEST))
    for slot in range(slots):
        here = pl.ds(pl.multiple_of((x ^ slot) * width, width), width)
        wide = dot(both, hi_ref[:, here], 1, 0)
        q = wide[:RANK] + wide[RANK:] + dot(p_hi, lo_ref[:, here], 1, 0)
        for j in range(tiles):
            out_ref[slot, j * RANK : (j + 1) * RANK, :] = q[:, j * LANES : (j + 1) * LANES]
        out_ref[slot, tiles * RANK :, :] = gram


def right_terms(p_sum, hi, lo, replicas, slots):
    height = hi.shape[1] // slots // LANES * RANK + 8
    return pl.pallas_call(
        functools.partial(right_kernel, replicas),
        in_specs=[WHOLE] * 3,
        out_specs=WHOLE,
        out_shape=jax.ShapeDtypeStruct((slots, height, LANES), F32),
        compiler_params=PARAMS,
        name="right_terms",
    )(p_sum, hi, lo)


def factor_kernel(sum_ref, out_ref):
    gram = unpack(sum_ref[sum_ref.shape[0] - 8 :, :])
    row = lax.broadcasted_iota(jnp.int32, (RANK, RANK), 0)
    column = lax.broadcasted_iota(jnp.int32, (RANK, RANK), 1)
    work = jnp.concatenate([gram, (row == column).astype(F32)], axis=1)
    below = lax.broadcasted_iota(jnp.int32, (RANK, 2 * RANK), 0)
    scale = jnp.zeros((RANK, 1), F32)
    first = lax.broadcasted_iota(jnp.int32, (RANK, 1), 0)
    for k in range(RANK):
        top = work[k : k + 1, :]
        pivot = work[k : k + 1, k : k + 1]
        scale = jnp.where(first == k, lax.rsqrt(pivot), scale)
        if k < RANK - 1:
            ratio = work[:, k : k + 1] * (1.0 / pivot)
            work = jnp.where(below > k, work - ratio * top, work)
    out_ref[...] = pack(work[:, RANK:] * scale)


def inverse_factor(total):
    return pl.pallas_call(
        factor_kernel,
        in_specs=[WHOLE],
        out_specs=WHOLE,
        out_shape=jax.ShapeDtypeStruct((8, LANES), F32),
        compiler_params=PARAMS,
        cost_estimate=pl.CostEstimate(flops=4_000_000, bytes_accessed=4_000_000, transcendentals=64),
        name="inverse_factor",
    )(total)


def hat_kernel(replicas, p_ref, inverse_ref, own_ref, other_ref):
    half = p_ref.shape[0] // 2
    inverse = unpack(inverse_ref[...])
    for i, out_ref in enumerate((own_ref, other_ref)):
        p = unpack_rows(p_ref[half * i : half * (i + 1)]) * (1.0 / replicas)
        out_ref[...] = pack_rows(dot(p, inverse, 1, 1, lax.Precision.HIGHEST))


def orthonormal(p_sum, inverse, replicas):
    half = jax.ShapeDtypeStruct((p_sum.shape[0] // 2, LANES), F32)
    return pl.pallas_call(
        functools.partial(hat_kernel, replicas),
        in_specs=[WHOLE] * 2,
        out_specs=[WHOLE] * 2,
        out_shape=[half, half],
        compiler_params=PARAMS,
        cost_estimate=pl.CostEstimate(flops=4_000_000, bytes_accessed=1_000_000, transcendentals=64),
        name="orthonormal",
    )(p_sum, inverse)


def side_kernel(replicas, own_ref, other_ref, hat_ref):
    rows = hat_ref.shape[1] - 16
    at = lax.broadcasted_iota(jnp.int32, (16, rows), 0) + lax.axis_index(("z", "y")) * (rows // replicas)
    chosen = (lax.broadcasted_iota(jnp.int32, (16, rows), 1) == at).astype(F32)
    for i, ref in enumerate((own_ref, other_ref)):
        hat = unpack_rows(ref[...])
        hat_ref[i, :rows] = left_three(hat)
        hat_ref[i, rows:] = left_three(dot(chosen, hat, 1, 0, lax.Precision.HIGHEST))


def left_sides(own, other, replicas):
    rows = 4 * own.shape[0]
    return pl.pallas_call(
        functools.partial(side_kernel, replicas),
        in_specs=[WHOLE] * 2,
        out_specs=WHOLE,
        out_shape=jax.ShapeDtypeStruct((2, rows + 16, 3 * RANK), BF16),
        compiler_params=PARAMS,
        cost_estimate=pl.CostEstimate(flops=4_000_000, bytes_accessed=1_000_000, transcendentals=64),
        name="left_sides",
    )(own, other)


def piece_kernel(replicas, a_ref, b_ref, inverse_ref, out_ref):
    inverse = unpack(inverse_ref[...]) * (1.0 / replicas)
    tiles = a_ref.shape[0] // RANK
    rows = a_ref[...] + b_ref[...]
    wide = jnp.concatenate([rows[j * RANK : (j + 1) * RANK] for j in range(tiles)], axis=1)
    q = dot(inverse, wide, 1, 0, lax.Precision.HIGHEST)
    for j in range(tiles):
        out_ref[j * RANK : (j + 1) * RANK, :] = q[:, j * LANES : (j + 1) * LANES]


def finished_piece(a, b, inverse, replicas):
    return pl.pallas_call(
        functools.partial(piece_kernel, replicas),
        in_specs=[WHOLE] * 3,
        out_specs=WHOLE,
        out_shape=jax.ShapeDtypeStruct(a.shape, F32),
        compiler_params=PARAMS,
        name="finished_piece",
    )(a, b, inverse)


def update_kernel(mine, pieces_ref, hat_ref, full_ref, m1_ref, m2_ref, *refs):
    err_hbm, n1_hbm, n2_hbm, up_hbm, q_hbm, err_ref, n1_ref, n2_ref, up_ref, q_ref, tile_ref, flat_ref, err_sem, sem = refs[-14:]
    slots, height, _ = pieces_ref.shape
    tiles = height // RANK
    width = tiles * LANES
    x, core = lax.axis_index("x"), lax.axis_index("c")
    i, m = (0, core) if mine else (1, 1 - core)
    copies = []
    for slot in range(slots):
        block = x ^ slot
        here = pl.ds(pl.multiple_of(block * width, width), width)
        q = jnp.concatenate([pieces_ref[slot, j * RANK : (j + 1) * RANK, :] for j in range(tiles)], axis=1)
        right = right_three(q)
        approx = dot(hat_ref[i], right, 1, 0)
        err_ref[slot] = full_ref[:, here] - approx[: full_ref.shape[0]]
        copies.append(pltpu.make_async_copy(err_ref.at[slot], err_hbm.at[0, m, :, here], err_sem.at[slot]))
        copies[-1].start()
        q_ref[:, here] = q
        state = approx[full_ref.shape[0] :]
        for j in range(tiles):
            tile_ref[block * tiles + j] = state[:8, j * LANES : (j + 1) * LANES]
    share = flat_ref.shape[0]
    for j in range(slots * tiles):
        flat_ref[:, j, :] = tile_ref[j, :share, :]
    flat = flat_ref[...].reshape(share * slots * tiles, LANES)
    n1 = 0.9 * m1_ref[m] + 0.1 * flat
    n2 = 0.95 * m2_ref[m] + 0.05 * flat * flat
    n1_ref[...] = n1
    n2_ref[...] = n2
    up_ref[...] = (n1 / (jnp.sqrt(n2) + 1e-08)).astype(BF16)
    for k, (here, there) in enumerate(((n1_ref, n1_hbm), (n2_ref, n2_hbm), (up_ref, up_hbm), (q_ref, q_hbm))):
        copies.append(pltpu.make_async_copy(here, there.at[m], sem.at[k]))
        copies[-1].start()
    for copy in copies:
        copy.wait()


def update(pieces, hat, full, moment1, moment2, mine, before=()):
    depth, columns = full.shape
    projections, slots = hat.shape[0], pieces.shape[0]
    state, tiles = moment1.shape[1], columns // LANES
    return pl.pallas_call(
        functools.partial(update_kernel, mine),
        in_specs=[WHOLE] * 5 + [AWAY] * len(before),
        out_specs=[AWAY] * 5,
        out_shape=[
            pltpu.HBM((1, projections, depth, columns), F32),
            pltpu.HBM(moment1.shape, F32),
            pltpu.HBM(moment2.shape, F32),
            pltpu.HBM(moment1.shape, BF16),
            pltpu.HBM((projections, RANK, columns), F32),
        ],
        scratch_shapes=[
            pltpu.VMEM((slots, depth, columns // slots), F32),
            pltpu.VMEM((state, LANES), F32),
            pltpu.VMEM((state, LANES), F32),
            pltpu.VMEM((state, LANES), BF16),
            pltpu.VMEM((RANK, columns), F32),
            pltpu.VMEM((tiles, 8, LANES), F32),
            pltpu.VMEM((state // tiles, tiles, LANES), F32),
            pltpu.SemaphoreType.DMA((slots,)),
            pltpu.SemaphoreType.DMA((4,)),
        ],
        input_output_aliases={5 + k: k for k in range(len(before))},
        compiler_params=PARAMS,
        cost_estimate=pl.CostEstimate(flops=100_000_000, bytes_accessed=4_000_000, transcendentals=30_000),
        name="update_own" if mine else "update_other",
    )(pieces, hat, full, moment1, moment2, *before)


def swap(value, axis, bit):
    return lax.ppermute(value, axis, [(i, i ^ bit) for i in range(lax.axis_size(axis))])


def four(values, axis):
    return (values[0] + swap(values[1], axis, 1)) + (swap(values[2], axis, 2) + swap(values[3], axis, 3))


def shards(grads, errors, q_prev, moment1, moment2):
    replicas, slots = lax.axis_size(("z", "y")), lax.axis_size("x")
    other_full, p_other, own_grads, own_errors, own_q = load(grads, errors, q_prev)
    own_full, p_own = left_own(own_grads, own_errors, own_q)
    p = jnp.concatenate([p_own, swap(p_other, "c", 1)])
    p, gift = lax.optimization_barrier((p, other_full))
    gift = swap(gift, "c", 1)
    p = four([p] * 4, "y")
    p = four([p] * 4, "z")
    far, hi, lo = lax.optimization_barrier((swap(p, "z", 6), *halves(own_full, gift)))
    p = p + far

    terms = right_terms(p, hi, lo, replicas, slots)
    total = four([terms[i] for i in range(slots)], "x")
    inverse = inverse_factor(total)
    q = four([total[:-8]] * 4, "y")
    q, inverse = lax.optimization_barrier((q, inverse))
    hat_own, hat_other = orthonormal(p, inverse, replicas)
    hat_gift = swap(hat_other, "c", 1)
    q = four([q] * 4, "z")
    q, hat_own, hat_gift = lax.optimization_barrier((q, hat_own, hat_gift))
    hat = left_sides(hat_own, hat_gift, replicas)
    far, hat = lax.optimization_barrier((swap(q, "z", 6), hat))
    piece = finished_piece(q, far, inverse, replicas)
    own = jnp.stack([piece] + [swap(piece, "x", i) for i in range(1, slots)])
    other = swap(own, "c", 1)
    done = update(own, hat, own_full, moment1, moment2, True)
    return tuple(update(other, hat, other_full, moment1, moment2, False, done))


def solution(mesh):
    mesh = Mesh(mesh.devices.reshape(8, 4, 4, 2), ("z", "y", "x", "c"))
    dp, fsdp = ("z", "y"), ("x", "c")
    blocks = P(dp, None, fsdp, None)
    states = P(None, fsdp + dp, None)
    return jax.shard_map(
        shards,
        mesh=mesh,
        in_specs=(blocks, blocks, P(), states, states),
        out_specs=(blocks, states, states, states, P()),
        check_vma=False,
    )
```
